128 devices in a mesh: sfc: 128 (over z, y, x, core).
Axes of the slice: x: 4, y: 4, z: 4, core: 2. Of those that a mesh axis runs over, the one named last changes fastest.
Arguments:
- state: float32 [5, 512, 16384], P(None, None, 'sfc'), as said below
- register: float32 [5, 512, 16384], P(None, None, 'sfc'), may hold values from -3 to 3
- metric: float32 [16384], P('sfc'), may hold values from 1 to 4
- counts: int32 [128], P('sfc'), may hold values from 96 to 128, as said below
- send_slots: int32 [16384, 16], P('sfc'), may hold values from 0 to 768, as said below
- mortar_refs: int32 [4096, 5], P('sfc'), may hold values from 0 to 2815, as said below
- face_refs: int32 [16384, 2], P('sfc'), may hold values from 0 to 2815, as said below
Outputs:
- state_next: float32 [5, 512, 16384], P(None, None, 'sfc')
- register_next: float32 [5, 512, 16384], P(None, None, 'sfc')
The draws below stay inside these ranges and needn't reach their ends.
Inputs may be any that keep to these rules, and one draw needn't show every extreme that they name: `counts`: at least 96; some device has exactly that many and some device is full. `send_slots`: row q * 128 + r lists face slots of live elements of device q whose traces device r needs, live entries first and 768 in the unused rest. Rows are nonempty only for r - q equal to 1, -1, 2, -2 or 128 / 2 modulo 128; each such row holds at least half of 16 live entries and every device fills one of its rows completely. No slot appears twice on a device. `mortar_refs`: each entry is a reference of the evaluating device that names a face slot of a live element; over all mortar_refs and face_refs, every face slot of the forest is named at most once, and every live entry of send_slots is named exactly once. `face_refs`: as for mortar_refs. `state`: density and pressure are positive.
All inputs are finite; a program needn't handle non-finite values.
Results may differ from the reference program's by a relative error of at most 0.0003.
Values sent between devices are 32-bit elements; how exact they have to be, the bound alone decides.
No kernel may reach another device: no remote copies, remote signals or barrier semaphores. Data moves between devices by JAX's collectives and lax.ppermute only.
A program may use at most 128 MiB of HBM per device.

```python
import math
import jax
import jax.numpy as jnp
import numpy as np
from jax import lax

E_DEV = 128
NODES = 512
BLK = 16
M_DEV = 32
F_DEV = 128
ELEMS = 16384
N_SFC = 128


def topology(key):
    devices = N_SFC
    elems = E_DEV
    slots = 6 * elems
    width = BLK
    total = 5 * M_DEV + 2 * F_DEV
    keys = jax.random.split(key, 7)
    index = jnp.arange(devices, dtype=jnp.int32)
    counts = jax.random.randint(keys[0], (devices,), 3 * elems // 4, elems + 1, dtype=jnp.int32)
    fullest = jax.random.randint(keys[1], (), 0, devices, dtype=jnp.int32)
    emptiest = (fullest + 1 + jax.random.randint(keys[2], (), 0, devices - 1, dtype=jnp.int32)) % devices
    counts = jnp.where(index == fullest, elems, jnp.where(index == emptiest, 3 * elems // 4, counts))
    ranks = jax.vmap(lambda sub: jax.random.permutation(sub, slots))(jax.random.split(keys[3], devices))
    dead = (jnp.arange(slots, dtype=jnp.int32)[None, :] % elems >= counts[:, None]).astype(jnp.int32)
    order = jnp.argsort(ranks.astype(jnp.int32) + dead * slots, axis=1).astype(jnp.int32)
    offsets = jnp.array([1, devices - 1, 2, devices - 2, devices // 2], jnp.int32)
    fill = jax.random.randint(keys[4], (devices, 5), max(1, width // 2), width + 1, dtype=jnp.int32)
    full_peer = jax.random.randint(keys[5], (devices,), 0, 5, dtype=jnp.int32)
    fill = jnp.where(jnp.arange(5, dtype=jnp.int32)[None, :] == full_peer[:, None], width, fill)
    position = jnp.arange(width, dtype=jnp.int32)
    chosen = order[:, :5 * width].reshape(devices, 5, width)
    blocks = jnp.where(position[None, None, :] < fill[:, :, None], chosen, slots)
    target = (index[:, None] + offsets[None, :]) % devices
    send = jnp.full((devices, devices, width), slots, jnp.int32)
    send = send.at[index[:, None], target].set(blocks)
    source = (index[:, None] - offsets[None, :]) % devices
    received = fill[source, jnp.arange(5, dtype=jnp.int32)[None, :]]
    refs_in = slots + source[:, :, None] * width + position[None, None, :]
    valid = position[None, None, :] < received[:, :, None]
    large_key = 5 * width + total + 1
    key_in = jnp.where(valid, jnp.arange(5 * width, dtype=jnp.int32).reshape(1, 5, width), large_key)
    own = order[:, 5 * width:5 * width + total]
    candidates = jnp.concatenate([refs_in.reshape(devices, 5 * width), own], axis=1)
    own_keys = jnp.broadcast_to(5 * width + jnp.arange(total, dtype=jnp.int32), (devices, total))
    sort_keys = jnp.concatenate([key_in.reshape(devices, 5 * width), own_keys], axis=1)
    picked = jnp.argsort(sort_keys, axis=1)[:, :total]
    selected = jnp.take_along_axis(candidates, picked, axis=1)
    shuffle = jax.vmap(lambda sub: jax.random.permutation(sub, total))(jax.random.split(keys[6], devices))
    refs = jnp.take_along_axis(selected, shuffle.astype(jnp.int32), axis=1).astype(jnp.int32)
    mortars = refs[:, :5 * M_DEV].reshape(devices * M_DEV, 5)
    faces = refs[:, 5 * M_DEV:].reshape(devices * F_DEV, 2)
    return (counts, send.reshape(devices * devices, width), mortars, faces)


def draw_counts(key, part):
    return topology(key)[0]


def draw_send_slots(key, part):
    return topology(key)[1]


def draw_mortar_refs(key, part):
    return topology(key)[2]


def draw_face_refs(key, part):
    return topology(key)[3]


def draw_state(key, part):
    key = jax.random.fold_in(key, 11)
    keys = jax.random.split(key, 8)
    shape = (NODES, ELEMS)
    density = jax.random.uniform(keys[0], shape, jnp.float32, 0.5, 2.0)
    velocity = jnp.clip(0.5 * jax.random.normal(keys[1], (3,) + shape, jnp.float32), -1.5, 1.5)
    press = jax.random.uniform(keys[2], shape, jnp.float32, 0.5, 2.0)
    column = jnp.arange(ELEMS, dtype=jnp.int32)
    device = jax.random.randint(keys[3], (), 0, N_SFC, dtype=jnp.int32)
    beginning = jax.random.randint(keys[4], (), 0, 3 * E_DEV // 4 - 1, dtype=jnp.int32)
    first_column = device * E_DEV + beginning
    fast_region = ((column >= first_column) & (column < first_column + 2))[None, :]
    amplitude = jax.random.uniform(keys[5], (), jnp.float32, 1.0, 2.0)
    sparse = jax.random.uniform(keys[6], shape, jnp.float32, 0.04, 0.08)
    heated = amplitude * jax.random.uniform(keys[7], shape, jnp.float32, 1.0, 2.0)
    density = jnp.where(fast_region, sparse, density)
    press = jnp.where(fast_region, heated, press)
    energy = press / 0.4 + 0.5 * density * jnp.sum(velocity * velocity, axis=0)
    return jnp.concatenate([density[None], density[None] * velocity, energy[None]], axis=0)


def level_of(stream_key, dims, cuts, least, high):
    gain, own = 1.0, jax.random.fold_in(stream_key, 6)
    for dim, shards_of in cuts:
        steps = jnp.exp(jax.random.uniform(jax.random.fold_in(own, dim), (shards_of,), jnp.float32, least / len(cuts), high / len(cuts)))
        gain = gain * jnp.repeat(steps, dims[dim] // shards_of).reshape([-1 if axis == dim else 1 for axis in range(len(dims))])
    return gain


def noise(stream_key, shape, scale, bound, cuts=(), kind=jnp.bfloat16):
    entries = scale * jax.random.normal(stream_key, shape, jnp.float32)
    if cuts:
        entries = entries * level_of(stream_key, shape, cuts, -0.22, 0.18)
    return jnp.clip(entries, -bound, bound).astype(kind)


def setup_inputs(seed: int = 0) -> dict:
    seeds = jax.random.split(jax.random.key(seed), 8)
    state = draw_state(jax.random.fold_in(seeds[7], 71), 0)
    register = noise(seeds[1], (5, NODES, ELEMS), 0.5, 3.0, ((2, 128),), jnp.float32)
    metric = jnp.clip(jnp.exp(math.log(4.0) - 1.3862944 * jax.random.uniform(seeds[2], (ELEMS,), jnp.float32) ** level_of(seeds[2], (ELEMS,), ((0, 128),), -0.2, 0.2)), 1.0, 4.0)
    counts = draw_counts(jax.random.fold_in(seeds[7], 71), 0)
    send_slots = draw_send_slots(jax.random.fold_in(seeds[7], 71), 0)
    mortar_refs = draw_mortar_refs(jax.random.fold_in(seeds[7], 71), 0)
    face_refs = draw_face_refs(jax.random.fold_in(seeds[7], 71), 0)
    return dict(state=state, register=register, metric=metric, counts=counts, send_slots=send_slots, mortar_refs=mortar_refs, face_refs=face_refs)


GAMMA = 1.4
LIFT = 28.0
COURANT = 0.02
SECTION_A = -0.4178904745
SECTION_B = 0.3792103129999
HIGHEST = lax.Precision.HIGHEST
GLL_NODES = (-1.0, -0.8717401485096066, -0.5917001814331423, -0.2092992179024789, 0.2092992179024789, 0.5917001814331423, 0.8717401485096066, 1.0)
GLL_WEIGHTS = (0.03571428571428571, 0.2107042271435061, 0.3411226924835044, 0.4124587946587038, 0.4124587946587038, 0.3411226924835044, 0.2107042271435061, 0.03571428571428571)

def interp_matrix(nodes, points):
    matrix = np.ones((len(points), len(nodes)))
    for source in range(len(nodes)):
        for other in range(len(nodes)):
            if other != source:
                matrix[:, source] *= (points - nodes[other]) / (nodes[source] - nodes[other])
    return matrix

def node_tables():
    number = 8
    nodes = np.array(GLL_NODES)
    weights = np.array(GLL_WEIGHTS)
    differ = nodes[:, None] - nodes[None, :] + np.eye(number)
    barycentric = 1.0 / np.prod(differ, axis=1)
    deriv = barycentric[None, :] / barycentric[:, None] / differ
    deriv = deriv * (1.0 - np.eye(number))
    deriv = deriv - np.eye(number) * deriv.sum(axis=1)[:, None]
    halves = [interp_matrix(nodes, (nodes - 1.0) / 2.0), interp_matrix(nodes, (nodes + 1.0) / 2.0)]
    backs = [0.5 * (half.T * weights[None, :]) / weights[:, None] for half in halves]
    project_cols = []
    back_rows = []
    for first in range(2):
        for second in range(2):
            project_cols.append(np.kron(halves[first], halves[second]).T)
            back_rows.append(np.kron(backs[first], backs[second]).T)
    project_stack = np.concatenate(project_cols, axis=1)
    back_stack = np.concatenate(back_rows, axis=0)
    return (jnp.asarray(deriv, jnp.float32), jnp.asarray(project_stack, jnp.float32), jnp.asarray(back_stack, jnp.float32))

def normal_flux(fields, normal):
    density, mom_one, mom_two, mom_three, energy = fields
    inverse = 1.0 / density
    kinetic = 0.5 * (mom_one * mom_one + mom_two * mom_two + mom_three * mom_three) * inverse
    press = (GAMMA - 1.0) * (energy - kinetic)
    flow = mom_one * normal[0] + mom_two * normal[1] + mom_three * normal[2]
    speed = flow * inverse
    return [flow, mom_one * speed + press * normal[0], mom_two * speed + press * normal[1], mom_three * speed + press * normal[2], (energy + press) * speed]

def wave_speed(cube):
    density, mom_one, mom_two, mom_three, energy = [cube[field] for field in range(5)]
    inverse = 1.0 / density
    square = mom_one * mom_one + mom_two * mom_two + mom_three * mom_three
    press = (GAMMA - 1.0) * (energy - 0.5 * square * inverse)
    return jnp.sqrt(square) * inverse + jnp.sqrt(GAMMA * press * inverse)

def volume_terms(cube, metric, deriv):
    fields = [cube[field] for field in range(5)]
    forms = ['ia,fabce->fibce', 'ib,fabce->faice', 'ic,fabce->fabie']
    total = jnp.zeros_like(cube)
    for axis in range(3):
        normal = tuple((1.0 if comp == axis else 0.0 for comp in range(3)))
        flux = jnp.stack(normal_flux(fields, normal))
        total = total + jnp.einsum(forms[axis], deriv, flux, precision=HIGHEST)
    return -metric * total

def face_tables(cube):
    tables = []
    for face in range(6):
        axis = face // 2
        side = face % 2
        layer = lax.index_in_dim(cube, 7 * side, axis + 1, keepdims=False)
        flat = layer.reshape(5, 64, layer.shape[-1])
        sign = 2.0 * side - 1.0
        normal = tuple((sign if comp == axis else 0.0 for comp in range(3)))
        flux = jnp.stack(normal_flux([flat[field] for field in range(5)], normal))
        both = jnp.concatenate([flat, flux], axis=0)
        tables.append(both.reshape(640, layer.shape[-1]).T)
    return jnp.concatenate(tables, axis=0)

def lift_faces(rhs_cube, corrections, metric):
    elems = metric.shape[0]
    for face in range(6):
        axis = face // 2
        side = face % 2
        block = corrections[face * elems:(face + 1) * elems]
        layer = block.T.reshape(5, 8, 8, elems)
        index = [slice(None)] * 5
        index[axis + 1] = 7 * side
        rhs_cube = rhs_cube.at[tuple(index)].add(-LIFT * metric * layer)
    return rhs_cube

def mortar_terms(rows, lam, project_stack, back_stack):
    number = rows.shape[0]
    large = rows[:, 0].reshape(number * 10, 64)
    spread = jnp.dot(large, project_stack, precision=HIGHEST).reshape(number, 10, 4, 64)
    spread = jnp.transpose(spread, (0, 2, 1, 3))
    small = rows[:, 1:].reshape(number, 4, 10, 64)
    star = 0.5 * (spread[:, :, 5:] - small[:, :, 5:]) - 0.5 * lam * (small[:, :, :5] - spread[:, :, :5])
    child = -star - small[:, :, 5:]
    folded = jnp.transpose(star, (0, 2, 1, 3)).reshape(number * 5, 256)
    large_corr = jnp.dot(folded, back_stack, precision=HIGHEST).reshape(number, 5, 64)
    large_corr = large_corr - rows[:, 0, 320:].reshape(number, 5, 64)
    joined = jnp.concatenate([large_corr[:, None], child], axis=1)
    return joined.reshape(number * 5, 320)

def face_terms(rows, lam):
    left = rows[:, 0]
    right = rows[:, 1]
    star = 0.5 * (left[:, 320:] - right[:, 320:]) - 0.5 * lam * (right[:, :320] - left[:, :320])
    return jnp.stack([star - left[:, 320:], -star - right[:, 320:]], axis=1).reshape(-1, 320)

def reference(state, register, metric, counts, send_slots, mortar_refs, face_refs):
    deriv, project_stack, back_stack = node_tables()
    devices = counts.shape[0]
    elems = metric.shape[0] // devices
    slots = 6 * elems
    width = send_slots.shape[1]
    cubes = jnp.moveaxis(state.reshape(5, 8, 8, 8, devices, elems), 4, 0)
    metrics = metric.reshape(devices, elems)

    def device_terms(args):
        cube, scale, count = args
        live = jnp.arange(elems, dtype=jnp.int32) < count
        volume = volume_terms(cube, scale, deriv)
        table = face_tables(cube)
        fastest = jnp.max(jnp.where(live, wave_speed(cube), jnp.float32(0.0)))
        return (volume, table, fastest)
    volumes, tables, fastest = lax.map(device_terms, (cubes, metrics, counts))
    lam = jnp.max(fastest)
    flat_tables = tables.reshape(devices * slots, 640)

    def to_global(refs, owner):
        remote = refs >= slots
        extra = refs - slots
        source = jnp.where(remote, extra // width, 0).astype(jnp.int32)
        place = jnp.where(remote, extra % width, 0).astype(jnp.int32)
        sent = send_slots[source * devices + owner, place]
        return jnp.where(remote, source * slots + sent, owner * slots + refs).astype(jnp.int32)
    per_mortar = mortar_refs.shape[0] // devices
    per_face = face_refs.shape[0] // devices
    owner_m = (jnp.arange(devices * per_mortar, dtype=jnp.int32) // per_mortar)[:, None]
    owner_f = (jnp.arange(devices * per_face, dtype=jnp.int32) // per_face)[:, None]
    global_m = to_global(mortar_refs, owner_m)
    global_f = to_global(face_refs, owner_f)
    corr_m = mortar_terms(flat_tables[global_m], lam, project_stack, back_stack)
    corr_f = face_terms(flat_tables[global_f], lam)
    corrections = jnp.zeros((devices * slots, 320), jnp.float32)
    corrections = corrections.at[global_m.reshape(-1)].add(corr_m)
    corrections = corrections.at[global_f.reshape(-1)].add(corr_f)
    corrections = corrections.reshape(devices, slots, 320)
    registers = jnp.moveaxis(register.reshape(5, 512, devices, elems), 2, 0)
    states = jnp.moveaxis(state.reshape(5, 512, devices, elems), 2, 0)
    step = COURANT / lam

    def finish(args):
        volume, corr, scale, count, old_register, old_state = args
        live = (jnp.arange(elems, dtype=jnp.int32) < count).astype(jnp.float32)
        rhs = lift_faces(volume, corr, scale).reshape(5, 512, elems) * live
        new_register = SECTION_A * old_register + step * rhs
        return (old_state + SECTION_B * new_register, new_register)
    new_states, new_registers = lax.map(finish, (volumes, corrections, metrics, counts, registers, states))
    state_next = jnp.moveaxis(new_states, 0, 2).reshape(5, 512, devices * elems)
    register_next = jnp.moveaxis(new_registers, 0, 2).reshape(5, 512, devices * elems)
    return (state_next, register_next)
```

```python
import functools
import jax
import jax.numpy as jnp
import numpy as np
from jax import lax
from jax.experimental import pallas as pl
from jax.experimental.pallas import tpu as pltpu
from jax.sharding import PartitionSpec as P

GAMMA = 1.4
LIFT = 28.0
COURANT = 0.02
SECTION_A = -0.4178904745
SECTION_B = 0.3792103129999
HIGHEST = lax.Precision.HIGHEST
F32 = jnp.float32
BF16 = jnp.bfloat16
ELEMS = 128
SLOTS = 6 * ELEMS
WIDTH = 16
PEERS = 5
MORTARS = 32
FACES = 128
ROWS = 320
GLL_NODES = (
    -1.0,
    -0.8717401485096066,
    -0.5917001814331423,
    -0.2092992179024789,
    0.2092992179024789,
    0.5917001814331423,
    0.8717401485096066,
    1.0,
)
GLL_WEIGHTS = (
    0.03571428571428571,
    0.2107042271435061,
    0.3411226924835044,
    0.4124587946587038,
    0.4124587946587038,
    0.3411226924835044,
    0.2107042271435061,
    0.03571428571428571,
)


def interp_matrix(nodes, points):
    matrix = np.ones((len(points), len(nodes)))
    for source in range(len(nodes)):
        for other in range(len(nodes)):
            if other != source:
                matrix[:, source] *= (points - nodes[other]) / (nodes[source] - nodes[other])
    return matrix


def node_tables():
    number = 8
    nodes = np.array(GLL_NODES)
    weights = np.array(GLL_WEIGHTS)
    differ = nodes[:, None] - nodes[None, :] + np.eye(number)
    barycentric = 1.0 / np.prod(differ, axis=1)
    deriv = barycentric[None, :] / barycentric[:, None] / differ
    deriv = deriv * (1.0 - np.eye(number))
    deriv = deriv - np.eye(number) * deriv.sum(axis=1)[:, None]
    halves = [interp_matrix(nodes, (nodes - 1.0) / 2.0), interp_matrix(nodes, (nodes + 1.0) / 2.0)]
    backs = [0.5 * (half.T * weights[None, :]) / weights[:, None] for half in halves]
    project = np.concatenate([np.kron(halves[c // 2], halves[c % 2]) for c in range(4)], axis=0)
    back = np.concatenate([np.kron(backs[c // 2], backs[c % 2]) for c in range(4)], axis=0)
    return (
        deriv.astype(np.float32),
        project.astype(np.float32),
        back.astype(np.float32),
        np.kron(np.eye(32), deriv).astype(np.float32),
    )


def pairings(devices):
    index = np.arange(devices)
    low = index % 4 < 2
    partners = [
        index ^ 1,
        np.where(index % 2 == 1, index + 1, index - 1) % devices,
        np.where(low, index + 2, index - 2) % devices,
        np.where(low, index - 2, index + 2) % devices,
        (index + devices // 2) % devices,
    ]
    return [[(int(d), int(p)) for d, p in enumerate(side)] for side in partners]


def partner_of(me, devices):
    odd = me % 2
    low = jnp.where(me % 4 < 2, 2, -2)
    steps = [1 - 2 * odd, 2 * odd - 1, low, -low, devices // 2]
    return [lax.rem(me + step + devices, devices) for step in steps]


def split3(value):
    high = value.astype(BF16)
    rest = value - high.astype(F32)
    mid = rest.astype(BF16)
    low = (rest - mid.astype(F32)).astype(BF16)
    return high, mid, low


def iota(shape, dim):
    return lax.broadcasted_iota(jnp.int32, shape, dim)


def dot_nt(left, right):
    return lax.dot_general(left, right, (((1,), (1,)), ((), ())), preferred_element_type=F32)


def one_hot(mask):
    return jnp.where(mask, F32(1.0), F32(0.0)).astype(BF16)


def thirds(value, size):
    return value[:size] + value[size : 2 * size] + value[2 * size : 3 * size]


def face_layer(ref, field, face):
    axis, side = face // 2, face % 2
    if axis == 0:
        return ref[field, 448 * side : 448 * side + 64, :]
    if axis == 1:
        return jnp.concatenate(
            [ref[field, a * 64 + 56 * side : a * 64 + 56 * side + 8, :] for a in range(8)], axis=0
        )
    return ref[field, pl.ds(7 * side, 64, stride=8), :]


def add_layer(ref, field, face, value):
    axis, side = face // 2, face % 2
    if axis == 0:
        ref[field, 448 * side : 448 * side + 64, :] += value
    elif axis == 1:
        for a in range(8):
            ref[field, a * 64 + 56 * side : a * 64 + 56 * side + 8, :] += value[8 * a : 8 * a + 8]
    else:
        place = pl.ds(7 * side, 64, stride=8)
        ref[field, place, :] = ref[field, place, :] + value


def out_columns(send_ref, partners):
    eye = iota((WIDTH, WIDTH), 0) == iota((WIDTH, WIDTH), 1)
    columns = []
    for peer in range(PEERS):
        row = send_ref[pl.ds(partners[peer], 1), :]
        columns.append(jnp.sum(jnp.where(eye, row, 0), axis=1, keepdims=True))
    columns.append(jnp.full((ELEMS - PEERS * WIDTH, 1), SLOTS, jnp.int32))
    return jnp.concatenate(columns, axis=0)


def ref_columns(mortar_ref, face_ref):
    large = mortar_ref[:, 0:1]
    return jnp.concatenate(
        [large] * 4 + [face_ref[:, 0:1]] + [mortar_ref[:, c : c + 1] for c in range(1, 5)] + [face_ref[:, 1:2]],
        axis=0,
    )


def remote_targets(partners):
    lane = iota((1, ELEMS), 1)
    target = jnp.full((1, ELEMS), -1, jnp.int32)
    for peer in range(PEERS):
        inside = (lane >= peer * WIDTH) & (lane < (peer + 1) * WIDTH)
        target = jnp.where(inside, SLOTS + partners[peer] * WIDTH + lane - peer * WIDTH, target)
    return target


def send_kernel(devices, state_ref, count_ref, send_ref, m0, m1, m2, m3, m4, split_ref, fast_ref):
    partners = partner_of(lax.axis_index("sfc"), devices)
    fastest = jnp.zeros((8, ELEMS), F32)
    for a in range(8):
        part = slice(64 * a, 64 * a + 64)
        density, one, two, three, energy = [state_ref[field, part, :] for field in range(5)]
        inverse = 1.0 / density
        square = one * one + two * two + three * three
        press = (GAMMA - 1.0) * (energy - 0.5 * square * inverse)
        speed = jnp.sqrt(square) * inverse + jnp.sqrt(GAMMA * press * inverse)
        fastest = jnp.maximum(fastest, jnp.max(speed.reshape(8, 8, ELEMS), axis=0))
    fastest = jnp.where(iota((8, ELEMS), 1) < count_ref[0], fastest, 0.0)
    fast_ref[...] = fastest
    for face in range(6):
        lanes = slice(face * ELEMS, (face + 1) * ELEMS)
        for field in range(5):
            parts = split3(face_layer(state_ref, field, face))
            for term in range(3):
                split_ref[term * ROWS + field * 64 : term * ROWS + field * 64 + 64, lanes] = parts[term]
    row = iota((16, SLOTS), 0)
    face = iota((16, SLOTS), 1) // ELEMS
    sign = jnp.where(face % 2 == 1, F32(1.0), F32(-1.0))
    split_ref[3 * ROWS : 3 * ROWS + 16, :] = jnp.where(row == face // 2, sign, 0.0).astype(BF16)
    chosen = one_hot(out_columns(send_ref, partners) == iota((ELEMS, SLOTS), 1))
    picked = dot_nt(split_ref[...], chosen)
    rows = jnp.concatenate(
        [thirds(picked, ROWS), picked[3 * ROWS : 3 * ROWS + 16], jnp.zeros((48, ELEMS), F32)], axis=0
    )
    message = rows.T
    for peer, ref in enumerate((m0, m1, m2, m3, m4)):
        ref[0:WIDTH, :] = message[peer * WIDTH : (peer + 1) * WIDTH]
        ref[WIDTH : WIDTH + 8, 0:ELEMS] = fastest
        ref[WIDTH : WIDTH + 8, ELEMS:] = jnp.zeros((8, 256), F32)


def local_kernel(deriv, state_ref, split_ref, mortar_ref, face_ref, mix_ref, gather_ref, volume_ref, fa, fb, fc):
    columns = ref_columns(mortar_ref, face_ref)
    chosen = one_hot(columns == iota((512, SLOTS), 1))
    picked = dot_nt(split_ref[...], chosen)
    gather_ref[0:ROWS, :] = thirds(picked, ROWS)
    gather_ref[ROWS : ROWS + 16, :] = picked[3 * ROWS : 3 * ROWS + 16]
    for a in range(8):
        part = slice(64 * a, 64 * a + 64)
        density, one, two, three, energy = [state_ref[field, part, :] for field in range(5)]
        inverse = 1.0 / density
        press = (GAMMA - 1.0) * (energy - 0.5 * (one * one + two * two + three * three) * inverse)
        total = energy + press
        for axis, ref in enumerate((fa, fb, fc)):
            flow = (one, two, three)[axis]
            speed = flow * inverse
            terms = [one * speed, two * speed, three * speed]
            terms[axis] = terms[axis] + press
            for field, value in enumerate([flow] + terms + [total * speed]):
                ref[field, part, :] = value

    def body(field, carry):
        for half in range(2):
            part = slice(256 * half, 256 * half + 256)
            volume_ref[field, part, :] = jnp.dot(
                mix_ref[...], fc[field, part, :], precision=HIGHEST, preferred_element_type=F32
            )
        for b in range(8):
            values = [fa[field, a * 64 + 8 * b : a * 64 + 8 * b + 8, :] for a in range(8)]
            for i in range(8):
                place = slice(i * 64 + 8 * b, i * 64 + 8 * b + 8)
                total = volume_ref[field, place, :]
                for j in range(8):
                    total = total + float(deriv[i, j]) * values[j]
                volume_ref[field, place, :] = total
        for a in range(8):
            values = [fb[field, a * 64 + 8 * b : a * 64 + 8 * b + 8, :] for b in range(8)]
            for i in range(8):
                place = slice(a * 64 + 8 * i, a * 64 + 8 * i + 8)
                total = volume_ref[field, place, :]
                for j in range(8):
                    total = total + float(deriv[i, j]) * values[j]
                volume_ref[field, place, :] = total
        return carry

    lax.fori_loop(0, 5, body, 0)


def trace_flux(fields, normal):
    density, one, two, three, energy = fields
    inverse = 1.0 / density
    press = (GAMMA - 1.0) * (energy - 0.5 * (one * one + two * two + three * three) * inverse)
    flow = one * normal[0] + two * normal[1] + three * normal[2]
    speed = flow * inverse
    return [
        flow,
        one * speed + press * normal[0],
        two * speed + press * normal[1],
        three * speed + press * normal[2],
        (energy + press) * speed,
    ]


def child_select(stack, index):
    lanes = slice(index * ELEMS, (index + 1) * ELEMS)
    lane = iota((64, ELEMS), 1)
    value = stack[192:256, lanes]
    for child in (2, 1, 0):
        value = jnp.where(lane < 32 * (child + 1), stack[64 * child : 64 * child + 64, lanes], value)
    return value


def by_child(matrix_ref, values):
    stack = jnp.dot(
        matrix_ref[...], jnp.concatenate(values, axis=1), precision=HIGHEST, preferred_element_type=F32
    )
    return [child_select(stack, index) for index in range(len(values))]


def face_kernel(
    devices, own_ref, gather_ref, i0, i1, i2, i3, i4, mortar_ref, face_ref, project_ref, back_ref,
    corr_ref, m0, m1, m2, m3, m4, fast_ref, pool_ref
):
    partners = partner_of(lax.axis_index("sfc"), devices)
    incoming = (i0, i1, i2, i3, i4)
    fast = own_ref[...]
    for ref in incoming[0:4]:
        fast = jnp.maximum(fast, ref[WIDTH : WIDTH + 8, 0:ELEMS])
    fast_ref[...] = fast
    columns = ref_columns(mortar_ref, face_ref)
    remote = one_hot(columns == remote_targets(partners))
    arrived = jnp.concatenate(
        [ref[0:WIDTH, :] for ref in incoming] + [jnp.zeros((ELEMS - PEERS * WIDTH, 384), F32)], axis=0
    ).T
    high, mid, low = split3(arrived[:ROWS])
    picked = dot_nt(jnp.concatenate([high, mid, low, arrived[ROWS : ROWS + 16].astype(BF16)], axis=0), remote)
    pool_ref[0:ROWS, :] = gather_ref[0:ROWS, :] + thirds(picked, ROWS)
    normals = gather_ref[ROWS : ROWS + 8, :] + picked[3 * ROWS : 3 * ROWS + 8]
    sides = []
    for side in range(4):
        lanes = slice(side * ELEMS, (side + 1) * ELEMS)
        fields = [pool_ref[64 * field : 64 * field + 64, lanes] for field in range(5)]
        normal = [normals[axis : axis + 1, lanes] for axis in range(3)]
        sides.append((fields, trace_flux(fields, normal)))
    (large_u, large_f), (left_u, left_f), (child_u, child_f), (right_u, right_f) = sides
    spread = by_child(project_ref, large_u + large_f)
    steady = [0.5 * (spread[5 + k] - child_f[k]) for k in range(5)]
    moving = [0.5 * (spread[k] - child_u[k]) for k in range(5)]
    folded = by_child(back_ref, steady + moving)
    for k in range(5):
        rows = slice(64 * k, 64 * k + 64)
        more = slice(ROWS + 64 * k, ROWS + 64 * k + 64)
        corr_ref[rows, 0:128] = folded[k] - 0.25 * large_f[k]
        corr_ref[more, 0:128] = folded[5 + k]
        corr_ref[rows, 256:384] = -steady[k] - child_f[k]
        corr_ref[more, 256:384] = -moving[k]
        even = 0.5 * (left_f[k] - right_f[k])
        jump = 0.5 * (left_u[k] - right_u[k])
        corr_ref[rows, 128:256] = even - left_f[k]
        corr_ref[more, 128:256] = jump
        corr_ref[rows, 384:512] = -even - right_f[k]
        corr_ref[more, 384:512] = -jump
    parts = split3(corr_ref[...])
    back = sum(jnp.dot(part, remote, preferred_element_type=F32) for part in parts).T
    for peer, ref in enumerate((m0, m1, m2, m3, m4)):
        ref[...] = back[peer * WIDTH : (peer + 1) * WIDTH]


def lift_kernel(
    corr_ref, mortar_ref, face_ref, volume_ref, register_ref, metric_ref, count_ref, steady_ref, rate_ref
):
    columns = ref_columns(mortar_ref, face_ref)
    chosen = one_hot(columns == iota((512, SLOTS), 1))
    live = iota((1, ELEMS), 1) < count_ref[0]
    scale = jnp.where(live, COURANT * metric_ref[...], 0.0)
    for field in range(5):
        steady_ref[field] = SECTION_A * register_ref[field]
        rate_ref[field] = -scale * volume_ref[field]
    parts = split3(corr_ref[...])
    layers = sum(jnp.dot(part, chosen, preferred_element_type=F32) for part in parts)
    lift = -LIFT * scale
    for face in range(6):
        lanes = slice(face * ELEMS, (face + 1) * ELEMS)
        for field in range(5):
            add_layer(rate_ref, field, face, lift * layers[64 * field : 64 * field + 64, lanes])
            add_layer(
                steady_ref, field, face, lift * layers[ROWS + 64 * field : ROWS + 64 * field + 64, lanes]
            )


def finish_kernel(
    devices, steady_ref, rate_ref, state_ref, i0, i1, i2, i3, i4, fast_ref, send_ref, metric_ref, count_ref,
    state_out, register_out
):
    partners = partner_of(lax.axis_index("sfc"), devices)
    lam = jnp.max(jnp.max(fast_ref[...], axis=0, keepdims=True), axis=1, keepdims=True)
    inverse = 1.0 / lam
    live = iota((1, ELEMS), 1) < count_ref[0]
    lift = jnp.where(live, -LIFT * COURANT * metric_ref[...], 0.0) * inverse
    chosen = one_hot(out_columns(send_ref, partners) == iota((ELEMS, SLOTS), 1))
    arrived = jnp.concatenate(
        [ref[:, 0:ROWS] + lam * ref[:, ROWS : 2 * ROWS] for ref in (i0, i1, i2, i3, i4)]
        + [jnp.zeros((ELEMS - PEERS * WIDTH, ROWS), F32)],
        axis=0,
    ).T
    layers = sum(jnp.dot(part, chosen, preferred_element_type=F32) for part in split3(arrived))
    for field in range(5):
        register_out[field] = steady_ref[field] + inverse * rate_ref[field]
    for face in range(6):
        lanes = slice(face * ELEMS, (face + 1) * ELEMS)
        for field in range(5):
            add_layer(register_out, field, face, lift * layers[64 * field : 64 * field + 64, lanes])
    for field in range(5):
        state_out[field] = state_ref[field] + SECTION_B * register_out[field]


VMEM = pl.BlockSpec(memory_space=pltpu.VMEM)
SMEM = pl.BlockSpec(memory_space=pltpu.SMEM)


def call(kernel, name, outs, specs, cost, scratch=()):
    return pl.pallas_call(
        kernel,
        name=name,
        out_shape=[jax.ShapeDtypeStruct(shape, dtype) for shape, dtype in outs],
        in_specs=specs,
        out_specs=[VMEM] * len(outs),
        scratch_shapes=list(scratch),
        compiler_params=pltpu.CompilerParams(vmem_limit_bytes=40 * 1024 * 1024),
        cost_estimate=pl.CostEstimate(flops=cost[0], bytes_accessed=cost[1], transcendentals=0),
    )


def per_device(state, register, metric, counts, send_slots, mortar_refs, face_refs):
    devices = lax.axis_size("sfc")
    deriv, project, back, mix = node_tables()
    metric = metric.reshape(1, ELEMS)
    pairs = pairings(devices)
    cube = (5, 512, ELEMS)
    first = call(
        functools.partial(send_kernel, devices), "send",
        [((WIDTH + 8, 384), F32)] * 5 + [((3 * ROWS + 16, SLOTS), BF16), ((8, ELEMS), F32)],
        [VMEM, SMEM, VMEM], (200_000_000, 3_000_000),
    )(state, counts, send_slots)
    messages, split, own = first[:5], first[5], first[6]
    incoming = [lax.ppermute(message, "sfc", pair) for message, pair in zip(messages, pairs)]
    gathered, volume = call(
        functools.partial(local_kernel, deriv), "local",
        [((ROWS + 16, 512), F32), (cube, F32)],
        [VMEM] * 5, (2_000_000_000, 5_000_000),
        [pltpu.VMEM(cube, F32)] * 3,
    )(state, split, mortar_refs, face_refs, jnp.asarray(mix))
    second = call(
        functools.partial(face_kernel, devices), "faces",
        [((2 * ROWS, 512), F32)] + [((WIDTH, 2 * ROWS), F32)] * 5 + [((8, ELEMS), F32)],
        [VMEM] * 11, (1_000_000_000, 3_000_000),
        [pltpu.VMEM((ROWS, 512), F32)],
    )(own, gathered, *incoming, mortar_refs, face_refs, jnp.asarray(project), jnp.asarray(back))
    corrections, replies, fast = second[0], second[1:6], second[6]
    returned = [lax.ppermute(reply, "sfc", pair) for reply, pair in zip(replies, pairs)]
    shift = 4
    while shift < devices:
        pair = [(d, d ^ shift) for d in range(devices)]
        fast = jnp.maximum(fast, lax.ppermute(fast, "sfc", pair))
        shift *= 2
    steady, rate = call(
        lift_kernel, "lift", [(cube, F32)] * 2, [VMEM] * 6 + [SMEM], (1_500_000_000, 6_000_000)
    )(corrections, mortar_refs, face_refs, volume, register, metric, counts)
    return tuple(
        call(
            functools.partial(finish_kernel, devices), "finish", [(cube, F32)] * 2,
            [VMEM] * 11 + [SMEM], (200_000_000, 6_000_000),
        )(steady, rate, state, *returned, fast, send_slots, metric, counts)
    )


def solution(mesh):
    return jax.shard_map(
        per_device,
        mesh=mesh,
        in_specs=(
            P(None, None, "sfc"),
            P(None, None, "sfc"),
            P("sfc"),
            P("sfc"),
            P("sfc", None),
            P("sfc", None),
            P("sfc", None),
        ),
        out_specs=(P(None, None, "sfc"), P(None, None, "sfc")),
        check_vma=False,
    )
```

```python
import functools
import jax
import jax.numpy as jnp
import numpy as np
from jax import lax
from jax.experimental import pallas as pl
from jax.experimental.pallas import tpu as pltpu
from jax.sharding import PartitionSpec as P

GAMMA = 1.4
LIFT = 28.0
COURANT = 0.02
SECTION_A = -0.4178904745
SECTION_B = 0.3792103129999
HIGHEST = lax.Precision.HIGHEST
F32 = jnp.float32
BF16 = jnp.bfloat16
ELEMS = 128
SLOTS = 6 * ELEMS
WIDTH = 16
PEERS = 5
MORTARS = 32
FACES = 128
ROWS = 320
GLL_NODES = (
    -1.0,
    -0.8717401485096066,
    -0.5917001814331423,
    -0.2092992179024789,
    0.2092992179024789,
    0.5917001814331423,
    0.8717401485096066,
    1.0,
)
GLL_WEIGHTS = (
    0.03571428571428571,
    0.2107042271435061,
    0.3411226924835044,
    0.4124587946587038,
    0.4124587946587038,
    0.3411226924835044,
    0.2107042271435061,
    0.03571428571428571,
)


def interp_matrix(nodes, points):
    matrix = np.ones((len(points), len(nodes)))
    for source in range(len(nodes)):
        for other in range(len(nodes)):
            if other != source:
                matrix[:, source] *= (points - nodes[other]) / (nodes[source] - nodes[other])
    return matrix


def node_tables():
    number = 8
    nodes = np.array(GLL_NODES)
    weights = np.array(GLL_WEIGHTS)
    differ = nodes[:, None] - nodes[None, :] + np.eye(number)
    barycentric = 1.0 / np.prod(differ, axis=1)
    deriv = barycentric[None, :] / barycentric[:, None] / differ
    deriv = deriv * (1.0 - np.eye(number))
    deriv = deriv - np.eye(number) * deriv.sum(axis=1)[:, None]
    halves = [interp_matrix(nodes, (nodes - 1.0) / 2.0), interp_matrix(nodes, (nodes + 1.0) / 2.0)]
    backs = [0.5 * (half.T * weights[None, :]) / weights[:, None] for half in halves]
    project = np.concatenate([np.kron(halves[c // 2], halves[c % 2]) for c in range(4)], axis=0)
    back = np.concatenate([np.kron(backs[c // 2], backs[c % 2]) for c in range(4)], axis=0)
    return (
        deriv.astype(np.float32),
        project.astype(np.float32),
        back.astype(np.float32),
        np.kron(np.eye(32), deriv).astype(np.float32),
    )


def pairings(devices):
    index = np.arange(devices)
    low = index % 4 < 2
    partners = [
        index ^ 1,
        np.where(index % 2 == 1, index + 1, index - 1) % devices,
        np.where(low, index + 2, index - 2) % devices,
        np.where(low, index - 2, index + 2) % devices,
        (index + devices // 2) % devices,
    ]
    return [[(int(d), int(p)) for d, p in enumerate(side)] for side in partners]


def partner_of(me, devices):
    odd = me % 2
    low = jnp.where(me % 4 < 2, 2, -2)
    steps = [1 - 2 * odd, 2 * odd - 1, low, -low, devices // 2]
    return [lax.rem(me + step + devices, devices) for step in steps]


def split3(value):
    high = value.astype(BF16)
    rest = value - high.astype(F32)
    mid = rest.astype(BF16)
    low = (rest - mid.astype(F32)).astype(BF16)
    return high, mid, low


def iota(shape, dim):
    return lax.broadcasted_iota(jnp.int32, shape, dim)


def dot_nt(left, right):
    return lax.dot_general(left, right, (((1,), (1,)), ((), ())), preferred_element_type=F32)


def one_hot(mask):
    return jnp.where(mask, F32(1.0), F32(0.0)).astype(BF16)


def thirds(value, size):
    return value[:size] + value[size : 2 * size] + value[2 * size : 3 * size]


def face_layer(ref, field, face):
    axis, side = face // 2, face % 2
    if axis == 0:
        return ref[field, 448 * side : 448 * side + 64, :]
    if axis == 1:
        return jnp.concatenate(
            [ref[field, a * 64 + 56 * side : a * 64 + 56 * side + 8, :] for a in range(8)], axis=0
        )
    return ref[field, pl.ds(7 * side, 64, stride=8), :]


def add_layer(ref, field, face, value):
    axis, side = face // 2, face % 2
    if axis == 0:
        ref[field, 448 * side : 448 * side + 64, :] += value
    elif axis == 1:
        for a in range(8):
            ref[field, a * 64 + 56 * side : a * 64 + 56 * side + 8, :] += value[8 * a : 8 * a + 8]
    else:
        place = pl.ds(7 * side, 64, stride=8)
        ref[field, place, :] = ref[field, place, :] + value


def out_columns(send_ref, partners):
    lane = iota((WIDTH, ELEMS), 1)
    slots = send_ref[...]
    columns = [
        jnp.sum(jnp.where(lane == partners[peer], slots, 0), axis=1, keepdims=True) for peer in range(PEERS)
    ]
    columns.append(jnp.full((ELEMS - PEERS * WIDTH, 1), SLOTS, jnp.int32))
    return jnp.concatenate(columns, axis=0)


def ref_rows(mortar_ref, face_ref):
    large = mortar_ref[0:1, :]
    return jnp.concatenate(
        [large] * 4 + [face_ref[0:1, :]] + [mortar_ref[c : c + 1, :] for c in range(1, 5)] + [face_ref[1:2, :]],
        axis=1,
    )


def own_choice(mortar_ref, face_ref):
    return one_hot(ref_rows(mortar_ref, face_ref) == iota((SLOTS, 512), 0))


def remote_choice(mortar_ref, face_ref, partners):
    place = iota((ELEMS, 1), 0)
    target = jnp.full((ELEMS, 1), -1, jnp.int32)
    for peer in range(PEERS):
        inside = (place >= peer * WIDTH) & (place < (peer + 1) * WIDTH)
        target = jnp.where(inside, SLOTS + partners[peer] * WIDTH + place - peer * WIDTH, target)
    return one_hot(ref_rows(mortar_ref, face_ref) == target)


def send_kernel(devices, state_ref, count_ref, send_ref, m0, m1, m2, m3, m4, split_ref, fast_ref):
    partners = partner_of(lax.axis_index("sfc"), devices)
    fastest = jnp.zeros((8, ELEMS), F32)
    for a in range(8):
        part = slice(64 * a, 64 * a + 64)
        density, one, two, three, energy = [state_ref[field, part, :] for field in range(5)]
        inverse = 1.0 / density
        square = one * one + two * two + three * three
        press = (GAMMA - 1.0) * (energy - 0.5 * square * inverse)
        speed = jnp.sqrt(square) * inverse + jnp.sqrt(GAMMA * press * inverse)
        fastest = jnp.maximum(fastest, jnp.max(speed.reshape(8, 8, ELEMS), axis=0))
    fastest = jnp.where(iota((8, ELEMS), 1) < count_ref[0], fastest, 0.0)
    fast_ref[...] = fastest
    for face in range(6):
        lanes = slice(face * ELEMS, (face + 1) * ELEMS)
        for field in range(5):
            parts = split3(face_layer(state_ref, field, face))
            for term in range(3):
                split_ref[term * ROWS + field * 64 : term * ROWS + field * 64 + 64, lanes] = parts[term]
    row = iota((16, SLOTS), 0)
    face = iota((16, SLOTS), 1) // ELEMS
    sign = jnp.where(face % 2 == 1, F32(1.0), F32(-1.0))
    split_ref[3 * ROWS : 3 * ROWS + 16, :] = jnp.where(row == face // 2, sign, 0.0).astype(BF16)
    chosen = one_hot(out_columns(send_ref, partners) == iota((ELEMS, SLOTS), 1))
    picked = dot_nt(split_ref[...], chosen)
    rows = jnp.concatenate(
        [thirds(picked, ROWS), picked[3 * ROWS : 3 * ROWS + 16], jnp.zeros((48, ELEMS), F32)], axis=0
    )
    message = rows.T
    for peer, ref in enumerate((m0, m1, m2, m3, m4)):
        ref[0:WIDTH, :] = message[peer * WIDTH : (peer + 1) * WIDTH]
        ref[WIDTH : WIDTH + 8, 0:ELEMS] = fastest
        ref[WIDTH : WIDTH + 8, ELEMS:] = jnp.zeros((8, 256), F32)


def axis_flux(state_ref, axis, ref):
    for a in range(8):
        part = slice(64 * a, 64 * a + 64)
        density, one, two, three, energy = [state_ref[field, part, :] for field in range(5)]
        inverse = 1.0 / density
        press = (GAMMA - 1.0) * (energy - 0.5 * (one * one + two * two + three * three) * inverse)
        flow = (one, two, three)[axis]
        speed = flow * inverse
        terms = [one * speed, two * speed, three * speed]
        terms[axis] = terms[axis] + press
        for field, value in enumerate([flow] + terms + [(energy + press) * speed]):
            ref[field, part, :] = value


def first_kernel(deriv, turn_ref, state_ref, volume_ref, flux):
    axis_flux(state_ref, 0, flux)

    def body(field, carry):
        for b in range(8):
            values = [flux[field, a * 64 + 8 * b : a * 64 + 8 * b + 8, :] for a in range(8)]
            for i in range(8):
                total = float(deriv[i, 0]) * values[0]
                for j in range(1, 8):
                    total = total + float(deriv[i, j]) * values[j]
                volume_ref[field, i * 64 + 8 * b : i * 64 + 8 * b + 8, :] = total
        return carry

    lax.fori_loop(0, 5, body, 0)


def second_kernel(deriv, turn_ref, state_ref, before_ref, volume_ref, flux):
    axis_flux(state_ref, 1, flux)

    def body(field, carry):
        for a in range(8):
            values = [flux[field, a * 64 + 8 * b : a * 64 + 8 * b + 8, :] for b in range(8)]
            for i in range(8):
                place = slice(a * 64 + 8 * i, a * 64 + 8 * i + 8)
                total = before_ref[field, place, :]
                for j in range(8):
                    total = total + float(deriv[i, j]) * values[j]
                volume_ref[field, place, :] = total
        return carry

    lax.fori_loop(0, 5, body, 0)


def third_kernel(turn_ref, state_ref, before_ref, split_ref, mortar_ref, face_ref, mix_ref, gather_ref, volume_ref, flux):
    axis_flux(state_ref, 2, flux)
    picked = jnp.dot(split_ref[...], own_choice(mortar_ref, face_ref), preferred_element_type=F32)
    gather_ref[0:ROWS, :] = thirds(picked, ROWS)
    gather_ref[ROWS : ROWS + 16, :] = picked[3 * ROWS : 3 * ROWS + 16]
    for half in range(2):
        part = slice(256 * half, 256 * half + 256)
        mixed = jnp.dot(
            mix_ref[...],
            jnp.concatenate([flux[field, part, :] for field in range(5)], axis=1),
            precision=HIGHEST,
            preferred_element_type=F32,
        )
        for field in range(5):
            volume_ref[field, part, :] = before_ref[field, part, :] + mixed[:, field * ELEMS : (field + 1) * ELEMS]


def trace_flux(fields, normal):
    density, one, two, three, energy = fields
    inverse = 1.0 / density
    press = (GAMMA - 1.0) * (energy - 0.5 * (one * one + two * two + three * three) * inverse)
    flow = one * normal[0] + two * normal[1] + three * normal[2]
    speed = flow * inverse
    return [
        flow,
        one * speed + press * normal[0],
        two * speed + press * normal[1],
        three * speed + press * normal[2],
        (energy + press) * speed,
    ]


def child_select(stack, index):
    lanes = slice(index * ELEMS, (index + 1) * ELEMS)
    lane = iota((64, ELEMS), 1)
    value = stack[192:256, lanes]
    for child in (2, 1, 0):
        value = jnp.where(lane < 32 * (child + 1), stack[64 * child : 64 * child + 64, lanes], value)
    return value


def by_child(matrix_ref, values):
    stack = jnp.dot(
        matrix_ref[...], jnp.concatenate(values, axis=1), precision=HIGHEST, preferred_element_type=F32
    )
    return [child_select(stack, index) for index in range(len(values))]


def face_kernel(
    devices, turn_ref, gather_ref, i0, i1, i2, i3, i4, mortar_ref, face_ref, project_ref, back_ref, corr_ref, pool_ref
):
    partners = partner_of(lax.axis_index("sfc"), devices)
    incoming = (i0, i1, i2, i3, i4)
    remote = remote_choice(mortar_ref, face_ref, partners)
    arrived = jnp.concatenate(
        [ref[0:WIDTH, :] for ref in incoming] + [jnp.zeros((ELEMS - PEERS * WIDTH, 384), F32)], axis=0
    ).T
    high, mid, low = split3(arrived[:ROWS])
    picked = jnp.dot(
        jnp.concatenate([high, mid, low, arrived[ROWS : ROWS + 16].astype(BF16)], axis=0),
        remote,
        preferred_element_type=F32,
    )
    pool_ref[0:ROWS, :] = gather_ref[0:ROWS, :] + thirds(picked, ROWS)
    normals = gather_ref[ROWS : ROWS + 8, :] + picked[3 * ROWS : 3 * ROWS + 8]
    sides = []
    for side in range(4):
        lanes = slice(side * ELEMS, (side + 1) * ELEMS)
        fields = [pool_ref[64 * field : 64 * field + 64, lanes] for field in range(5)]
        normal = [normals[axis : axis + 1, lanes] for axis in range(3)]
        sides.append((fields, trace_flux(fields, normal)))
    (large_u, large_f), (left_u, left_f), (child_u, child_f), (right_u, right_f) = sides
    spread = by_child(project_ref, large_u + large_f)
    steady = [0.5 * (spread[5 + k] - child_f[k]) for k in range(5)]
    moving = [0.5 * (spread[k] - child_u[k]) for k in range(5)]
    folded = by_child(back_ref, steady + moving)
    for k in range(5):
        rows = slice(64 * k, 64 * k + 64)
        more = slice(ROWS + 64 * k, ROWS + 64 * k + 64)
        corr_ref[rows, 0:128] = folded[k] - 0.25 * large_f[k]
        corr_ref[more, 0:128] = folded[5 + k]
        corr_ref[rows, 256:384] = -steady[k] - child_f[k]
        corr_ref[more, 256:384] = -moving[k]
        even = 0.5 * (left_f[k] - right_f[k])
        jump = 0.5 * (left_u[k] - right_u[k])
        corr_ref[rows, 128:256] = even - left_f[k]
        corr_ref[more, 128:256] = jump
        corr_ref[rows, 384:512] = -even - right_f[k]
        corr_ref[more, 384:512] = -jump


def reply_kernel(devices, corr_ref, mortar_ref, face_ref, turn_ref, last_ref, m0, m1, m2, m3, m4, fast_ref):
    partners = partner_of(lax.axis_index("sfc"), devices)
    remote = remote_choice(mortar_ref, face_ref, partners)
    fast = jnp.maximum(turn_ref[...], last_ref[...])
    fast_ref[...] = fast
    back = sum(dot_nt(part, remote) for part in split3(corr_ref[...])).T
    for peer, ref in enumerate((m0, m1, m2, m3, m4)):
        ref[0:WIDTH, :] = back[peer * WIDTH : (peer + 1) * WIDTH]
        ref[WIDTH : WIDTH + 8, 0:ELEMS] = fast
        ref[WIDTH : WIDTH + 8, ELEMS:] = jnp.zeros((8, 512), F32)


def lift_kernel(
    turn_ref, corr_ref, mortar_ref, face_ref, volume_ref, register_ref, metric_ref, count_ref, steady_ref, rate_ref
):
    chosen = own_choice(mortar_ref, face_ref)
    live = iota((1, ELEMS), 1) < count_ref[0]
    scale = jnp.where(live, COURANT * metric_ref[...], 0.0)
    for field in range(5):
        steady_ref[field] = SECTION_A * register_ref[field]
        rate_ref[field] = -scale * volume_ref[field]
    parts = split3(corr_ref[...])
    layers = sum(dot_nt(part, chosen) for part in parts)
    lift = -LIFT * scale
    for face in range(6):
        lanes = slice(face * ELEMS, (face + 1) * ELEMS)
        for field in range(5):
            add_layer(rate_ref, field, face, lift * layers[64 * field : 64 * field + 64, lanes])
            add_layer(
                steady_ref, field, face, lift * layers[ROWS + 64 * field : ROWS + 64 * field + 64, lanes]
            )


def finish_kernel(
    devices, steady_ref, rate_ref, state_ref, i0, i1, i2, i3, i4, fast_ref, send_ref, metric_ref, count_ref,
    state_out, register_out
):
    partners = partner_of(lax.axis_index("sfc"), devices)
    fast = fast_ref[...]
    for ref in (i0, i1, i2, i3):
        fast = jnp.maximum(fast, ref[WIDTH : WIDTH + 8, 0:ELEMS])
    lam = jnp.max(jnp.max(fast, axis=0, keepdims=True), axis=1, keepdims=True)
    inverse = 1.0 / lam
    live = iota((1, ELEMS), 1) < count_ref[0]
    lift = jnp.where(live, -LIFT * COURANT * metric_ref[...], 0.0) * inverse
    chosen = one_hot(out_columns(send_ref, partners) == iota((ELEMS, SLOTS), 1))
    arrived = jnp.concatenate(
        [ref[0:WIDTH, 0:ROWS] + lam * ref[0:WIDTH, ROWS : 2 * ROWS] for ref in (i0, i1, i2, i3, i4)]
        + [jnp.zeros((ELEMS - PEERS * WIDTH, ROWS), F32)],
        axis=0,
    ).T
    layers = sum(jnp.dot(part, chosen, preferred_element_type=F32) for part in split3(arrived))
    for field in range(5):
        register_out[field] = steady_ref[field] + inverse * rate_ref[field]
    for face in range(6):
        lanes = slice(face * ELEMS, (face + 1) * ELEMS)
        for field in range(5):
            add_layer(register_out, field, face, lift * layers[64 * field : 64 * field + 64, lanes])
    for field in range(5):
        state_out[field] = state_ref[field] + SECTION_B * register_out[field]


VMEM = pl.BlockSpec(memory_space=pltpu.VMEM)
SMEM = pl.BlockSpec(memory_space=pltpu.SMEM)


def call(kernel, name, outs, specs, cost, scratch=()):
    return pl.pallas_call(
        kernel,
        name=name,
        out_shape=[jax.ShapeDtypeStruct(shape, dtype) for shape, dtype in outs],
        in_specs=specs,
        out_specs=[VMEM] * len(outs),
        scratch_shapes=list(scratch),
        compiler_params=pltpu.CompilerParams(vmem_limit_bytes=40 * 1024 * 1024),
        cost_estimate=pl.CostEstimate(flops=cost[0], bytes_accessed=cost[1], transcendentals=0),
    )


def per_device(state, register, metric, counts, send_slots, mortar_refs, face_refs):
    devices = lax.axis_size("sfc")
    deriv, project, back, mix = node_tables()
    metric = metric.reshape(1, ELEMS)
    sends, mortars, faces = send_slots.T, mortar_refs.T, face_refs.T
    pairs = pairings(devices)
    cube = (5, 512, ELEMS)
    flux = [pltpu.VMEM(cube, F32)]

    def exchange(value, shift):
        return lax.ppermute(value, "sfc", [(d, d ^ shift) for d in range(devices)])

    first = call(
        functools.partial(send_kernel, devices), "send",
        [((WIDTH + 8, 384), F32)] * 5 + [((3 * ROWS + 16, SLOTS), BF16), ((8, ELEMS), F32)],
        [VMEM, SMEM, VMEM], (200_000_000, 3_000_000),
    )(state, counts, sends)
    messages, split, fast = first[:5], first[5], first[6]
    far = lax.ppermute(messages[4], "sfc", pairs[4])
    near = [lax.ppermute(message, "sfc", pair) for message, pair in zip(messages[:4], pairs[:4])]
    fast = jnp.maximum(fast, far[WIDTH : WIDTH + 8, 0:ELEMS])
    came = exchange(fast, 32)
    (volume,) = call(
        functools.partial(first_kernel, deriv), "volume_first", [(cube, F32)], [VMEM] * 2,
        (1_000_000_000, 2_600_000), flux,
    )(fast, state)
    fast = jnp.maximum(fast, came)
    came = exchange(fast, 16)
    (volume,) = call(
        functools.partial(second_kernel, deriv), "volume_second", [(cube, F32)], [VMEM] * 3,
        (1_000_000_000, 3_900_000), flux,
    )(fast, state, volume)
    fast = jnp.maximum(fast, came)
    came = exchange(fast, 8)
    gathered, volume = call(
        third_kernel, "volume_third_gather", [((ROWS + 16, 512), F32), (cube, F32)], [VMEM] * 7,
        (2_000_000_000, 6_000_000), flux,
    )(fast, state, volume, split, mortars, faces, jnp.asarray(mix))
    fast = jnp.maximum(fast, came)
    came = exchange(fast, 4)
    (corrections,) = call(
        functools.partial(face_kernel, devices), "faces", [((2 * ROWS, 512), F32)], [VMEM] * 11,
        (1_000_000_000, 3_000_000), [pltpu.VMEM((ROWS, 512), F32)],
    )(fast, gathered, *near, far, mortars, faces, jnp.asarray(project), jnp.asarray(back))
    second = call(
        functools.partial(reply_kernel, devices), "reply",
        [((WIDTH + 8, 2 * ROWS), F32)] * 5 + [((8, ELEMS), F32)],
        [VMEM] * 5, (500_000_000, 2_000_000),
    )(corrections, mortars, faces, fast, came)
    replies, fast = second[:5], second[5]
    returned = [lax.ppermute(reply, "sfc", pair) for reply, pair in zip(replies, pairs)]
    steady, rate = call(
        lift_kernel, "lift", [(cube, F32)] * 2, [VMEM] * 7 + [SMEM], (1_500_000_000, 6_000_000)
    )(fast, corrections, mortars, faces, volume, register, metric, counts)
    return tuple(
        call(
            functools.partial(finish_kernel, devices), "finish", [(cube, F32)] * 2,
            [VMEM] * 11 + [SMEM], (200_000_000, 6_000_000),
        )(steady, rate, state, *returned, fast, sends, metric, counts)
    )


def solution(mesh):
    return jax.shard_map(
        per_device,
        mesh=mesh,
        in_specs=(
            P(None, None, "sfc"),
            P(None, None, "sfc"),
            P("sfc"),
            P("sfc"),
            P("sfc", None),
            P("sfc", None),
            P("sfc", None),
        ),
        out_specs=(P(None, None, "sfc"), P(None, None, "sfc")),
        check_vma=False,
    )
```

```python
import functools
import jax
import jax.numpy as jnp
import numpy as np
from jax import lax
from jax.experimental import pallas as pl
from jax.experimental.pallas import tpu as pltpu
from jax.sharding import PartitionSpec as P

GAMMA = 1.4
LIFT = 28.0
COURANT = 0.02
SECTION_A = -0.4178904745
SECTION_B = 0.3792103129999
HIGHEST = lax.Precision.HIGHEST
F32 = jnp.float32
BF16 = jnp.bfloat16
ELEMS = 128
SLOTS = 6 * ELEMS
WIDTH = 16
PEERS = 5
MORTARS = 32
FACES = 128
ROWS = 320
GLL_NODES = (
    -1.0,
    -0.8717401485096066,
    -0.5917001814331423,
    -0.2092992179024789,
    0.2092992179024789,
    0.5917001814331423,
    0.8717401485096066,
    1.0,
)
GLL_WEIGHTS = (
    0.03571428571428571,
    0.2107042271435061,
    0.3411226924835044,
    0.4124587946587038,
    0.4124587946587038,
    0.3411226924835044,
    0.2107042271435061,
    0.03571428571428571,
)


def interp_matrix(nodes, points):
    matrix = np.ones((len(points), len(nodes)))
    for source in range(len(nodes)):
        for other in range(len(nodes)):
            if other != source:
                matrix[:, source] *= (points - nodes[other]) / (nodes[source] - nodes[other])
    return matrix


def node_tables():
    number = 8
    nodes = np.array(GLL_NODES)
    weights = np.array(GLL_WEIGHTS)
    differ = nodes[:, None] - nodes[None, :] + np.eye(number)
    barycentric = 1.0 / np.prod(differ, axis=1)
    deriv = barycentric[None, :] / barycentric[:, None] / differ
    deriv = deriv * (1.0 - np.eye(number))
    deriv = deriv - np.eye(number) * deriv.sum(axis=1)[:, None]
    halves = [interp_matrix(nodes, (nodes - 1.0) / 2.0), interp_matrix(nodes, (nodes + 1.0) / 2.0)]
    backs = [0.5 * (half.T * weights[None, :]) / weights[:, None] for half in halves]
    project = np.concatenate([np.kron(halves[c // 2], halves[c % 2]) for c in range(4)], axis=0)
    back = np.concatenate([np.kron(backs[c // 2], backs[c % 2]) for c in range(4)], axis=0)
    return (
        deriv.astype(np.float32),
        project.astype(np.float32),
        back.astype(np.float32),
        np.kron(np.eye(32), deriv).astype(np.float32),
    )


def pairings(devices):
    index = np.arange(devices)
    low = index % 4 < 2
    y = index // 8 % 4
    partners = dict(
        chip=index ^ 1,
        pair=np.where(low, index + 2, index - 2) % devices,
        next=np.where(low, index - 2, index + 2) % devices,
        far=(index + devices // 2) % devices,
        y_first=index ^ 8,
        y_second=index + 8 * (np.where(y % 2 == 1, y + 1, y - 1) % 4 - y),
        z_first=index ^ 32,
    )
    return {name: [(int(d), int(p)) for d, p in enumerate(side)] for name, side in partners.items()}


def partner_of(me, devices):
    odd = me % 2
    low = jnp.where(me % 4 < 2, 2, -2)
    steps = [1 - 2 * odd, 2 * odd - 1, low, -low, devices // 2]
    return [lax.rem(me + step + devices, devices) for step in steps]


def split3(value):
    high = value.astype(BF16)
    rest = value - high.astype(F32)
    mid = rest.astype(BF16)
    low = (rest - mid.astype(F32)).astype(BF16)
    return high, mid, low


def split2(value):
    high = value.astype(BF16)
    return high, (value - high.astype(F32)).astype(BF16)


def stack_terms(matrix):
    high = matrix.astype(BF16)
    mid = (matrix - high.astype(np.float32)).astype(BF16)
    return jnp.asarray(np.concatenate([high, high, mid, mid], axis=1))


def iota(shape, dim):
    return lax.broadcasted_iota(jnp.int32, shape, dim)


def dot_nt(left, right):
    return lax.dot_general(left, right, (((1,), (1,)), ((), ())), preferred_element_type=F32)


def one_hot(mask):
    return jnp.where(mask, F32(1.0), F32(0.0)).astype(BF16)


def thirds(value, size):
    return value[:size] + value[size : 2 * size] + value[2 * size : 3 * size]


def face_layer(ref, field, face):
    axis, side = face // 2, face % 2
    if axis == 0:
        return ref[field, 448 * side : 448 * side + 64, :]
    if axis == 1:
        return jnp.concatenate(
            [ref[field, a * 64 + 56 * side : a * 64 + 56 * side + 8, :] for a in range(8)], axis=0
        )
    return ref[field, pl.ds(7 * side, 64, stride=8), :]


def add_layer(ref, field, face, value):
    axis, side = face // 2, face % 2
    if axis == 0:
        ref[field, 448 * side : 448 * side + 64, :] += value
    elif axis == 1:
        for a in range(8):
            ref[field, a * 64 + 56 * side : a * 64 + 56 * side + 8, :] += value[8 * a : 8 * a + 8]
    else:
        place = pl.ds(7 * side, 64, stride=8)
        ref[field, place, :] = ref[field, place, :] + value


def out_columns(slots_ref, partners):
    lane = iota((WIDTH, ELEMS), 1)
    slots = slots_ref[...]
    columns = [
        jnp.sum(jnp.where(lane == partners[peer], slots, 0), axis=1, keepdims=True) for peer in range(PEERS)
    ]
    columns.append(jnp.full((ELEMS - PEERS * WIDTH, 1), SLOTS, jnp.int32))
    return jnp.concatenate(columns, axis=0)


def ref_rows(mortar_ref, face_ref):
    large = mortar_ref[0:1, :]
    return jnp.concatenate(
        [large] * 4 + [face_ref[0:1, :]] + [mortar_ref[c : c + 1, :] for c in range(1, 5)] + [face_ref[1:2, :]],
        axis=1,
    )


def own_choice(mortar_ref, face_ref):
    return one_hot(ref_rows(mortar_ref, face_ref) == iota((SLOTS, 512), 0))


def remote_choice(mortar_ref, face_ref, partners):
    place = iota((ELEMS, 1), 0)
    target = jnp.full((ELEMS, 1), -1, jnp.int32)
    for peer in range(PEERS):
        inside = (place >= peer * WIDTH) & (place < (peer + 1) * WIDTH)
        target = jnp.where(inside, SLOTS + partners[peer] * WIDTH + place - peer * WIDTH, target)
    return one_hot(ref_rows(mortar_ref, face_ref) == target)


def table_kernel(state_ref, split_ref, speed_ref):
    fastest = jnp.zeros((8, ELEMS), F32)
    for a in range(8):
        part = slice(64 * a, 64 * a + 64)
        density, one, two, three, energy = [state_ref[field, part, :] for field in range(5)]
        inverse = 1.0 / density
        square = one * one + two * two + three * three
        press = (GAMMA - 1.0) * (energy - 0.5 * square * inverse)
        speed = jnp.sqrt(square) * inverse + jnp.sqrt(GAMMA * press * inverse)
        fastest = jnp.maximum(fastest, jnp.max(speed.reshape(8, 8, ELEMS), axis=0))
    speed_ref[...] = fastest
    for face in range(6):
        lanes = slice(face * ELEMS, (face + 1) * ELEMS)
        for field in range(5):
            parts = split3(face_layer(state_ref, field, face))
            for term in range(3):
                split_ref[term * ROWS + field * 64 : term * ROWS + field * 64 + 64, lanes] = parts[term]
    row = iota((16, SLOTS), 0)
    face = iota((16, SLOTS), 1) // ELEMS
    sign = jnp.where(face % 2 == 1, F32(1.0), F32(-1.0))
    split_ref[3 * ROWS : 3 * ROWS + 16, :] = jnp.where(row == face // 2, sign, 0.0).astype(BF16)


def send_kernel(
    devices, split_ref, speed_ref, count_ref, slots_ref, metric_ref, chip_ref, raw_ref, fast_ref, scale_ref
):
    partners = partner_of(lax.axis_index("sfc"), devices)
    live = iota((8, ELEMS), 1) < count_ref[0]
    scale_ref[...] = jnp.where(live, COURANT * metric_ref[...], 0.0)
    fastest = jnp.max(jnp.where(live, speed_ref[...], 0.0), axis=0, keepdims=True)
    fastest = jnp.max(fastest, axis=1, keepdims=True)
    fast_ref[...] = jnp.broadcast_to(fastest, (8, ELEMS))
    chosen = one_hot(out_columns(slots_ref, partners) == iota((ELEMS, SLOTS), 1))
    picked = dot_nt(split_ref[...], chosen)
    rows = jnp.concatenate(
        [thirds(picked, ROWS), picked[3 * ROWS : 3 * ROWS + 16], jnp.broadcast_to(fastest, (48, ELEMS))], axis=0
    )
    message = rows.T
    chip_ref[...] = message[0 : 2 * WIDTH]
    raw_ref[...] = message[2 * WIDTH : 5 * WIDTH]


def pair_kernel(raw_ref, chip_ref, fast_ref, pair_ref, next_ref, best_ref):
    best = jnp.maximum(fast_ref[...], chip_ref[0:8, 256:384])
    best_ref[...] = best
    for k, ref in enumerate((pair_ref, next_ref)):
        ref[0:WIDTH, :] = raw_ref[k * WIDTH : (k + 1) * WIDTH, :]
        ref[WIDTH : 2 * WIDTH, :] = chip_ref[WIDTH : 2 * WIDTH, :]
    pair_ref[0:8, 256:384] = jnp.where(iota((8, ELEMS), 1) < 80, raw_ref[0:8, 256:384], best)


def far_kernel(turn_ref, raw_ref, pair_ref, fast_ref, far_ref, best_ref):
    best = jnp.maximum(fast_ref[...], pair_ref[0:8, 256:384])
    best_ref[...] = best
    far_ref[...] = raw_ref[2 * WIDTH : 3 * WIDTH, :]
    far_ref[0:8, 256:384] = jnp.where(iota((8, ELEMS), 1) < 80, raw_ref[2 * WIDTH : 2 * WIDTH + 8, 256:384], best)


def gather_blocks(devices, chip_ref, pair_ref, next_ref, far_ref, columns):
    place = lax.axis_index("sfc") % 4
    first = slice(0, WIDTH)
    second = slice(WIDTH, 2 * WIDTH)
    passed = jnp.where((place == 0) | (place == 3), next_ref[second, columns], pair_ref[second, columns])
    return [chip_ref[first, columns], passed, pair_ref[first, columns], next_ref[first, columns], far_ref[first, columns]]


def axis_flux(state_ref, axis, ref):
    for a in range(8):
        part = slice(64 * a, 64 * a + 64)
        density, one, two, three, energy = [state_ref[field, part, :] for field in range(5)]
        inverse = 1.0 / density
        press = (GAMMA - 1.0) * (energy - 0.5 * (one * one + two * two + three * three) * inverse)
        flow = (one, two, three)[axis]
        speed = flow * inverse
        terms = [one * speed, two * speed, three * speed]
        terms[axis] = terms[axis] + press
        for field, value in enumerate([flow] + terms + [(energy + press) * speed]):
            ref[field, part, :] = value


def first_kernel(deriv, turn_ref, state_ref, volume_ref, flux):
    axis_flux(state_ref, 0, flux)

    def body(field, carry):
        for b in range(8):
            values = [flux[field, a * 64 + 8 * b : a * 64 + 8 * b + 8, :] for a in range(8)]
            for i in range(8):
                total = float(deriv[i, 0]) * values[0]
                for j in range(1, 8):
                    total = total + float(deriv[i, j]) * values[j]
                volume_ref[field, i * 64 + 8 * b : i * 64 + 8 * b + 8, :] = total
        return carry

    lax.fori_loop(0, 5, body, 0)


def second_kernel(deriv, turn_ref, state_ref, before_ref, volume_ref, flux):
    axis_flux(state_ref, 1, flux)

    def body(field, carry):
        for a in range(8):
            values = [flux[field, a * 64 + 8 * b : a * 64 + 8 * b + 8, :] for b in range(8)]
            for i in range(8):
                place = slice(a * 64 + 8 * i, a * 64 + 8 * i + 8)
                total = before_ref[field, place, :]
                for j in range(8):
                    total = total + float(deriv[i, j]) * values[j]
                volume_ref[field, place, :] = total
        return carry

    lax.fori_loop(0, 5, body, 0)


def gather_kernel(split_ref, mortar_ref, face_ref, gather_ref):
    picked = jnp.dot(split_ref[...], own_choice(mortar_ref, face_ref), preferred_element_type=F32)
    gather_ref[0:ROWS, :] = thirds(picked, ROWS)
    gather_ref[ROWS : ROWS + 16, :] = picked[3 * ROWS : 3 * ROWS + 16]


def third_kernel(turn_ref, state_ref, before_ref, mix_ref, volume_ref, flux):
    axis_flux(state_ref, 2, flux)
    for half in range(2):
        part = slice(256 * half, 256 * half + 256)
        mixed = jnp.dot(
            mix_ref[...],
            jnp.concatenate([flux[field, part, :] for field in range(5)], axis=1),
            precision=HIGHEST,
            preferred_element_type=F32,
        )
        for field in range(5):
            volume_ref[field, part, :] = before_ref[field, part, :] + mixed[:, field * ELEMS : (field + 1) * ELEMS]


def trace_flux(fields, normal):
    density, one, two, three, energy = fields
    inverse = 1.0 / density
    press = (GAMMA - 1.0) * (energy - 0.5 * (one * one + two * two + three * three) * inverse)
    flow = one * normal[0] + two * normal[1] + three * normal[2]
    speed = flow * inverse
    return [
        flow,
        one * speed + press * normal[0],
        two * speed + press * normal[1],
        three * speed + press * normal[2],
        (energy + press) * speed,
    ]


def child_select(stack, index):
    lanes = slice(index * ELEMS, (index + 1) * ELEMS)
    lane = iota((64, ELEMS), 1)
    value = stack[192:256, lanes]
    for child in (2, 1, 0):
        value = jnp.where(lane < 32 * (child + 1), stack[64 * child : 64 * child + 64, lanes], value)
    return value


def by_child(matrix_ref, values):
    high, mid = split2(jnp.concatenate(values, axis=1))
    stack = jnp.dot(
        matrix_ref[...], jnp.concatenate([high, mid, high, mid], axis=0), preferred_element_type=F32
    )
    return [child_select(stack, index) for index in range(len(values))]


def face_kernel(
    devices, turn_ref, gather_ref, i0, i2, i3, i4, mortar_ref, face_ref, project_ref, back_ref,
    corr_ref, chip_ref, raw_ref, pool_ref
):
    partners = partner_of(lax.axis_index("sfc"), devices)
    incoming = gather_blocks(devices, i0, i2, i3, i4, slice(0, 384))
    remote = remote_choice(mortar_ref, face_ref, partners)
    arrived = jnp.concatenate(
        incoming + [jnp.zeros((ELEMS - PEERS * WIDTH, 384), F32)], axis=0
    ).T
    high, mid, low = split3(arrived[:ROWS])
    picked = jnp.dot(
        jnp.concatenate([high, mid, low, arrived[ROWS : ROWS + 16].astype(BF16)], axis=0),
        remote,
        preferred_element_type=F32,
    )
    pool_ref[0:ROWS, :] = gather_ref[0:ROWS, :] + thirds(picked, ROWS)
    normals = gather_ref[ROWS : ROWS + 8, :] + picked[3 * ROWS : 3 * ROWS + 8]
    sides = []
    for side in range(4):
        lanes = slice(side * ELEMS, (side + 1) * ELEMS)
        fields = [pool_ref[64 * field : 64 * field + 64, lanes] for field in range(5)]
        normal = [normals[axis : axis + 1, lanes] for axis in range(3)]
        sides.append((fields, trace_flux(fields, normal)))
    (large_u, large_f), (left_u, left_f), (child_u, child_f), (right_u, right_f) = sides
    spread = by_child(project_ref, large_u + large_f)
    steady = [0.5 * (spread[5 + k] - child_f[k]) for k in range(5)]
    moving = [0.5 * (spread[k] - child_u[k]) for k in range(5)]
    folded = by_child(back_ref, steady + moving)
    for k in range(5):
        rows = slice(64 * k, 64 * k + 64)
        more = slice(ROWS + 64 * k, ROWS + 64 * k + 64)
        corr_ref[rows, 0:128] = folded[k] - 0.25 * large_f[k]
        corr_ref[more, 0:128] = folded[5 + k]
        corr_ref[rows, 256:384] = -steady[k] - child_f[k]
        corr_ref[more, 256:384] = -moving[k]
        even = 0.5 * (left_f[k] - right_f[k])
        jump = 0.5 * (left_u[k] - right_u[k])
        corr_ref[rows, 128:256] = even - left_f[k]
        corr_ref[more, 128:256] = jump
        corr_ref[rows, 384:512] = -even - right_f[k]
        corr_ref[more, 384:512] = -jump
    back = sum(dot_nt(part, remote) for part in split3(corr_ref[...])).T
    chip_ref[...] = back[0 : 2 * WIDTH]
    raw_ref[...] = back[2 * WIDTH : 5 * WIDTH]


def reply_kernel(turn_ref, last_ref, raw_ref, chip_ref, pair_ref, next_ref, far_ref, best_ref):
    best = jnp.maximum(turn_ref[...], last_ref[...])
    best_ref[...] = best
    pair_ref[0:WIDTH, 0 : 2 * ROWS] = raw_ref[0:WIDTH, :]
    next_ref[0:WIDTH, 0 : 2 * ROWS] = raw_ref[WIDTH : 2 * WIDTH, :]
    far_ref[:, 0 : 2 * ROWS] = raw_ref[2 * WIDTH : 3 * WIDTH, :]
    for ref in (pair_ref, next_ref):
        ref[WIDTH : 2 * WIDTH, 0 : 2 * ROWS] = chip_ref[WIDTH : 2 * WIDTH, :]
    for ref in (pair_ref, next_ref, far_ref):
        for k in range(ref.shape[0] // 8):
            ref[8 * k : 8 * k + 8, 2 * ROWS :] = best


def lift_kernel(
    turn_ref, corr_ref, mortar_ref, face_ref, volume_ref, register_ref, scale_ref, steady_ref, rate_ref
):
    chosen = own_choice(mortar_ref, face_ref)
    scale = scale_ref[0:1, :]
    for field in range(5):
        steady_ref[field] = SECTION_A * register_ref[field]
        rate_ref[field] = -scale * volume_ref[field]
    parts = split3(corr_ref[...])
    layers = sum(dot_nt(part, chosen) for part in parts)
    lift = -LIFT * scale
    for face in range(6):
        lanes = slice(face * ELEMS, (face + 1) * ELEMS)
        for field in range(5):
            add_layer(rate_ref, field, face, lift * layers[64 * field : 64 * field + 64, lanes])
            add_layer(
                steady_ref, field, face, lift * layers[ROWS + 64 * field : ROWS + 64 * field + 64, lanes]
            )


def finish_kernel(
    devices, steady_ref, rate_ref, state_ref, i0, i2, i3, i4, fast_ref, slots_ref, scale_ref,
    state_hbm, register_hbm, state_out, register_out, sems
):
    partners = partner_of(lax.axis_index("sfc"), devices)
    fast = fast_ref[...]
    for ref in (i2, i3, i4):
        fast = jnp.maximum(fast, ref[0:8, 2 * ROWS :])
    fast = jnp.where(iota((8, ELEMS), 1) < 80, 0.0, fast)
    lam = jnp.max(jnp.max(fast, axis=0, keepdims=True), axis=1, keepdims=True)
    inverse = 1.0 / lam
    lift = -LIFT * scale_ref[0:1, :] * inverse
    chosen = one_hot(out_columns(slots_ref, partners) == iota((ELEMS, SLOTS), 1))
    arrived = jnp.concatenate(
        [
            block[:, 0:ROWS] + lam * block[:, ROWS : 2 * ROWS]
            for block in gather_blocks(devices, i0, i2, i3, i4, slice(0, 2 * ROWS))
        ]
        + [jnp.zeros((ELEMS - PEERS * WIDTH, ROWS), F32)],
        axis=0,
    ).T
    parts = jnp.concatenate(split3(arrived), axis=0)
    layers = thirds(jnp.dot(parts, chosen, preferred_element_type=F32), ROWS)
    copies = []
    for field in range(5):
        register_out[field] = steady_ref[field] + inverse * rate_ref[field]
        for face in range(6):
            lanes = slice(face * ELEMS, (face + 1) * ELEMS)
            add_layer(register_out, field, face, lift * layers[64 * field : 64 * field + 64, lanes])
        copies.append(pltpu.make_async_copy(register_out.at[field], register_hbm.at[field], sems.at[2 * field]))
        copies[-1].start()
        state_out[field] = state_ref[field] + SECTION_B * register_out[field]
        copies.append(pltpu.make_async_copy(state_out.at[field], state_hbm.at[field], sems.at[2 * field + 1]))
        copies[-1].start()
    for copy in copies:
        copy.wait()


VMEM = pl.BlockSpec(memory_space=pltpu.VMEM)
SMEM = pl.BlockSpec(memory_space=pltpu.SMEM)
HBM = pl.BlockSpec(memory_space=pltpu.HBM)


def call(kernel, name, outs, specs, cost, scratch=(), out_specs=None):
    return pl.pallas_call(
        kernel,
        name=name,
        out_shape=[jax.ShapeDtypeStruct(shape, dtype) for shape, dtype in outs],
        in_specs=specs,
        out_specs=out_specs or [VMEM] * len(outs),
        scratch_shapes=list(scratch),
        compiler_params=pltpu.CompilerParams(vmem_limit_bytes=40 * 1024 * 1024),
        cost_estimate=pl.CostEstimate(flops=cost[0], bytes_accessed=cost[1], transcendentals=0),
    )


def per_device(state, register, metric, counts, send_slots, mortar_refs, face_refs):
    devices = lax.axis_size("sfc")
    deriv, project, back, mix = node_tables()
    metric = metric.reshape(1, ELEMS)
    sends, mortars, faces = send_slots.T, mortar_refs.T, face_refs.T
    pairs = pairings(devices)
    cube = (5, 512, ELEMS)
    flux = [pltpu.VMEM(cube, F32)]

    def exchange(value, name):
        return lax.ppermute(value, "sfc", pairs[name])

    one, two, three = [((k * WIDTH, 384), F32) for k in (1, 2, 3)]
    row = ((8, ELEMS), F32)
    split, speed = call(
        table_kernel, "table", [((3 * ROWS + 16, SLOTS), BF16), row], [VMEM], (100_000_000, 3_000_000)
    )(state)
    chip, raw, fast, scale = call(
        functools.partial(send_kernel, devices), "send", [two, three, row, row], [VMEM] * 2 + [SMEM] + [VMEM] * 2,
        (200_000_000, 2_000_000),
    )(split, speed, counts, sends, metric)
    chip = exchange(chip, "chip")
    pair, onward, fast = call(pair_kernel, "pair", [two, two, row], [VMEM] * 3, (0, 200_000))(raw, chip, fast)
    onward = exchange(onward, "next")
    pair = exchange(pair, "pair")
    (gathered,) = call(
        gather_kernel, "gather", [((ROWS + 16, 512), F32)], [VMEM] * 3, (1_000_000_000, 2_000_000)
    )(split, mortars, faces)
    far, fast = call(far_kernel, "far", [one, row], [VMEM] * 4, (0, 200_000))(gathered, raw, pair, fast)
    far = exchange(far, "far")
    fast = jnp.maximum(fast, far[0:8, 256:384])
    came = exchange(fast, "y_first")
    (volume,) = call(
        functools.partial(first_kernel, deriv), "volume_first", [(cube, F32)], [VMEM] * 2,
        (1_000_000_000, 2_600_000), flux,
    )(fast, state)
    fast = jnp.maximum(fast, came)
    came = exchange(fast, "y_second")
    corrections, chip, raw = call(
        functools.partial(face_kernel, devices), "faces",
        [((2 * ROWS, 512), F32), ((2 * WIDTH, 2 * ROWS), F32), ((3 * WIDTH, 2 * ROWS), F32)],
        [VMEM] * 10, (1_000_000_000, 3_000_000), [pltpu.VMEM((ROWS, 512), F32)],
    )(fast, gathered, chip, pair, onward, far, mortars, faces, stack_terms(project), stack_terms(back))
    fast = jnp.maximum(fast, came)
    came = exchange(fast, "z_first")
    chip = exchange(chip, "chip")
    (volume,) = call(
        functools.partial(second_kernel, deriv), "volume_second", [(cube, F32)], [VMEM] * 3,
        (1_000_000_000, 3_900_000), flux,
    )(fast, state, volume)
    wide = 2 * ROWS + ELEMS
    pair, onward, far, fast = call(
        reply_kernel, "reply",
        [((2 * WIDTH, wide), F32)] * 2 + [((WIDTH, wide), F32), row], [VMEM] * 4, (0, 500_000),
    )(fast, came, raw, chip)
    onward = exchange(onward, "next")
    far = exchange(far, "far")
    pair = exchange(pair, "pair")
    (volume,) = call(
        third_kernel, "volume_third", [(cube, F32)], [VMEM] * 4, (1_000_000_000, 6_000_000), flux,
    )(fast, state, volume, jnp.asarray(mix))
    steady, rate = call(
        lift_kernel, "lift", [(cube, F32)] * 2, [VMEM] * 7, (1_500_000_000, 6_000_000)
    )(fast, corrections, mortars, faces, volume, register, scale)
    return tuple(
        call(
            functools.partial(finish_kernel, devices), "finish", [(cube, F32)] * 2,
            [VMEM] * 10, (200_000_000, 6_000_000),
            [pltpu.VMEM(cube, F32)] * 2 + [pltpu.SemaphoreType.DMA((10,))], [HBM] * 2,
        )(steady, rate, state, chip, pair, onward, far, fast, sends, scale)
    )


def solution(mesh):
    return jax.shard_map(
        per_device,
        mesh=mesh,
        in_specs=(
            P(None, None, "sfc"),
            P(None, None, "sfc"),
            P("sfc"),
            P("sfc"),
            P("sfc", None),
            P("sfc", None),
            P("sfc", None),
        ),
        out_specs=(P(None, None, "sfc"), P(None, None, "sfc")),
        check_vma=False,
    )
```

```python
import functools
import jax
import jax.numpy as jnp
import numpy as np
from jax import lax
from jax.experimental import pallas as pl
from jax.experimental.pallas import tpu as pltpu
from jax.sharding import PartitionSpec as P

GAMMA = 1.4
LIFT = 28.0
COURANT = 0.02
SECTION_A = -0.4178904745
SECTION_B = 0.3792103129999
HIGHEST = lax.Precision.HIGHEST
F32 = jnp.float32
BF16 = jnp.bfloat16
ELEMS = 128
SLOTS = 6 * ELEMS
WIDTH = 16
PEERS = 5
MORTARS = 32
FACES = 128
ROWS = 320
GLL_NODES = (
    -1.0,
    -0.8717401485096066,
    -0.5917001814331423,
    -0.2092992179024789,
    0.2092992179024789,
    0.5917001814331423,
    0.8717401485096066,
    1.0,
)
GLL_WEIGHTS = (
    0.03571428571428571,
    0.2107042271435061,
    0.3411226924835044,
    0.4124587946587038,
    0.4124587946587038,
    0.3411226924835044,
    0.2107042271435061,
    0.03571428571428571,
)


def interp_matrix(nodes, points):
    matrix = np.ones((len(points), len(nodes)))
    for source in range(len(nodes)):
        for other in range(len(nodes)):
            if other != source:
                matrix[:, source] *= (points - nodes[other]) / (nodes[source] - nodes[other])
    return matrix


def node_tables():
    number = 8
    nodes = np.array(GLL_NODES)
    weights = np.array(GLL_WEIGHTS)
    differ = nodes[:, None] - nodes[None, :] + np.eye(number)
    barycentric = 1.0 / np.prod(differ, axis=1)
    deriv = barycentric[None, :] / barycentric[:, None] / differ
    deriv = deriv * (1.0 - np.eye(number))
    deriv = deriv - np.eye(number) * deriv.sum(axis=1)[:, None]
    halves = [interp_matrix(nodes, (nodes - 1.0) / 2.0), interp_matrix(nodes, (nodes + 1.0) / 2.0)]
    backs = [0.5 * (half.T * weights[None, :]) / weights[:, None] for half in halves]
    project = np.concatenate([np.kron(halves[c // 2], halves[c % 2]) for c in range(4)], axis=0)
    back = np.concatenate([np.kron(backs[c // 2], backs[c % 2]) for c in range(4)], axis=0)
    return (
        deriv.astype(np.float32),
        project.astype(np.float32),
        back.astype(np.float32),
        np.kron(np.eye(32), deriv).astype(np.float32),
    )


def pairings(devices):
    index = np.arange(devices)
    low = index % 4 < 2
    y = index // 8 % 4
    partners = dict(
        chip=index ^ 1,
        pair=np.where(low, index + 2, index - 2) % devices,
        next=np.where(low, index - 2, index + 2) % devices,
        far=(index + devices // 2) % devices,
        y_first=index ^ 9,
        y_second=(index + 8 * (np.where(y % 2 == 1, y + 1, y - 1) % 4 - y)) ^ 1,
        z_first=index ^ 33,
    )
    return {name: [(int(d), int(p)) for d, p in enumerate(side)] for name, side in partners.items()}


def partner_of(me, devices):
    odd = me % 2
    low = jnp.where(me % 4 < 2, 2, -2)
    steps = [1 - 2 * odd, 2 * odd - 1, low, -low, devices // 2]
    return [lax.rem(me + step + devices, devices) for step in steps]


def split3(value):
    high = value.astype(BF16)
    rest = value - high.astype(F32)
    mid = rest.astype(BF16)
    low = (rest - mid.astype(F32)).astype(BF16)
    return high, mid, low


def split2(value):
    high = value.astype(BF16)
    return high, (value - high.astype(F32)).astype(BF16)


def stack_terms(matrix):
    high = matrix.astype(BF16)
    mid = (matrix - high.astype(np.float32)).astype(BF16)
    return jnp.asarray(np.concatenate([high, high, mid, mid], axis=1))


def iota(shape, dim):
    return lax.broadcasted_iota(jnp.int32, shape, dim)


def dot_nt(left, right):
    return lax.dot_general(left, right, (((1,), (1,)), ((), ())), preferred_element_type=F32)


def one_hot(mask):
    return jnp.where(mask, F32(1.0), F32(0.0)).astype(BF16)


def thirds(value, size):
    return value[:size] + value[size : 2 * size] + value[2 * size : 3 * size]


def face_layer(ref, field, face):
    axis, side = face // 2, face % 2
    if axis == 0:
        return ref[field, 448 * side : 448 * side + 64, :]
    if axis == 1:
        return jnp.concatenate(
            [ref[field, a * 64 + 56 * side : a * 64 + 56 * side + 8, :] for a in range(8)], axis=0
        )
    return ref[field, pl.ds(7 * side, 64, stride=8), :]


def add_layer(ref, field, face, value):
    axis, side = face // 2, face % 2
    if axis == 0:
        ref[field, 448 * side : 448 * side + 64, :] += value
    elif axis == 1:
        for a in range(8):
            ref[field, a * 64 + 56 * side : a * 64 + 56 * side + 8, :] += value[8 * a : 8 * a + 8]
    else:
        place = pl.ds(7 * side, 64, stride=8)
        ref[field, place, :] = ref[field, place, :] + value


def out_columns(slots_ref, partners):
    lane = iota((WIDTH, ELEMS), 1)
    slots = slots_ref[...]
    columns = [
        jnp.sum(jnp.where(lane == partners[peer], slots, 0), axis=1, keepdims=True) for peer in range(PEERS)
    ]
    columns.append(jnp.full((ELEMS - PEERS * WIDTH, 1), SLOTS, jnp.int32))
    return jnp.concatenate(columns, axis=0)


def ref_rows(mortar_ref, face_ref):
    large = mortar_ref[0:1, :]
    return jnp.concatenate(
        [large] * 4 + [face_ref[0:1, :]] + [mortar_ref[c : c + 1, :] for c in range(1, 5)] + [face_ref[1:2, :]],
        axis=1,
    )


def own_choice(mortar_ref, face_ref):
    return one_hot(ref_rows(mortar_ref, face_ref) == iota((SLOTS, 512), 0))


def remote_choice(mortar_ref, face_ref, partners):
    place = iota((ELEMS, 1), 0)
    target = jnp.full((ELEMS, 1), -1, jnp.int32)
    for peer in range(PEERS):
        inside = (place >= peer * WIDTH) & (place < (peer + 1) * WIDTH)
        target = jnp.where(inside, SLOTS + partners[peer] * WIDTH + place - peer * WIDTH, target)
    return one_hot(ref_rows(mortar_ref, face_ref) == target)


def table_kernel(state_ref, split_ref, speed_ref):
    fastest = jnp.zeros((8, ELEMS), F32)
    for a in range(8):
        part = slice(64 * a, 64 * a + 64)
        density, one, two, three, energy = [state_ref[field, part, :] for field in range(5)]
        inverse = 1.0 / density
        square = one * one + two * two + three * three
        press = (GAMMA - 1.0) * (energy - 0.5 * square * inverse)
        speed = jnp.sqrt(square) * inverse + jnp.sqrt(GAMMA * press * inverse)
        fastest = jnp.maximum(fastest, jnp.max(speed.reshape(8, 8, ELEMS), axis=0))
    speed_ref[...] = fastest
    for face in range(6):
        lanes = slice(face * ELEMS, (face + 1) * ELEMS)
        for field in range(5):
            parts = split3(face_layer(state_ref, field, face))
            for term in range(3):
                split_ref[term * ROWS + field * 64 : term * ROWS + field * 64 + 64, lanes] = parts[term]
    row = iota((16, SLOTS), 0)
    face = iota((16, SLOTS), 1) // ELEMS
    sign = jnp.where(face % 2 == 1, F32(1.0), F32(-1.0))
    split_ref[3 * ROWS : 3 * ROWS + 16, :] = jnp.where(row == face // 2, sign, 0.0).astype(BF16)


def send_kernel(
    devices, split_ref, speed_ref, count_ref, slots_ref, metric_ref, chip_ref, raw_ref, fast_ref, scale_ref, chosen_ref
):
    partners = partner_of(lax.axis_index("sfc"), devices)
    live = iota((8, ELEMS), 1) < count_ref[...]
    scale_ref[...] = jnp.where(live, COURANT * metric_ref[...], 0.0)
    fastest = jnp.max(jnp.where(live, speed_ref[...], 0.0), axis=0, keepdims=True)
    fastest = jnp.max(fastest, axis=1, keepdims=True)
    fast_ref[...] = jnp.broadcast_to(fastest, (8, ELEMS))
    chosen = one_hot(out_columns(slots_ref, partners) == iota((ELEMS, SLOTS), 1))
    chosen_ref[...] = chosen
    picked = dot_nt(split_ref[...], chosen)
    rows = jnp.concatenate(
        [thirds(picked, ROWS), picked[3 * ROWS : 3 * ROWS + 16], jnp.broadcast_to(fastest, (48, ELEMS))], axis=0
    )
    message = rows.T
    chip_ref[...] = message[0 : 2 * WIDTH]
    raw_ref[...] = message[2 * WIDTH : 5 * WIDTH]


def relay_kernel(raw_ref, chip_ref, fast_ref, next_ref, far_ref, best_ref):
    best = jnp.maximum(fast_ref[...], chip_ref[0:8, 256:384])
    best_ref[...] = best
    next_ref[0:WIDTH, :] = raw_ref[WIDTH : 2 * WIDTH, :]
    next_ref[WIDTH : 2 * WIDTH, :] = chip_ref[WIDTH : 2 * WIDTH, :]
    far_ref[...] = raw_ref[2 * WIDTH : 3 * WIDTH, :]
    far_ref[0:8, 256:384] = jnp.where(iota((8, ELEMS), 1) < 80, raw_ref[2 * WIDTH : 2 * WIDTH + 8, 256:384], best)


def pair_kernel(turn_ref, raw_ref, chip_ref, far_ref, fast_ref, pair_ref, best_ref):
    best = jnp.maximum(fast_ref[...], far_ref[0:8, 256:384])
    best_ref[...] = best
    pair_ref[0:WIDTH, :] = raw_ref[0:WIDTH, :]
    pair_ref[WIDTH : 2 * WIDTH, :] = chip_ref[WIDTH : 2 * WIDTH, :]
    pair_ref[0:8, 256:384] = jnp.where(iota((8, ELEMS), 1) < 80, raw_ref[0:8, 256:384], best)


def gather_blocks(devices, chip_ref, pair_ref, next_ref, far_ref, columns):
    place = lax.axis_index("sfc") % 4
    first = slice(0, WIDTH)
    second = slice(WIDTH, 2 * WIDTH)
    passed = jnp.where((place == 0) | (place == 3), next_ref[second, columns], pair_ref[second, columns])
    return [chip_ref[first, columns], passed, pair_ref[first, columns], next_ref[first, columns], far_ref[first, columns]]


def axis_flux(state_ref, axis, ref):
    for a in range(8):
        part = slice(64 * a, 64 * a + 64)
        density, one, two, three, energy = [state_ref[field, part, :] for field in range(5)]
        inverse = 1.0 / density
        press = (GAMMA - 1.0) * (energy - 0.5 * (one * one + two * two + three * three) * inverse)
        flow = (one, two, three)[axis]
        speed = flow * inverse
        terms = [one * speed, two * speed, three * speed]
        terms[axis] = terms[axis] + press
        for field, value in enumerate([flow] + terms + [(energy + press) * speed]):
            ref[field, part, :] = value


def first_kernel(deriv, turn_ref, state_ref, volume_ref, flux):
    axis_flux(state_ref, 0, flux)

    def body(field, carry):
        for b in range(8):
            values = [flux[field, a * 64 + 8 * b : a * 64 + 8 * b + 8, :] for a in range(8)]
            for i in range(8):
                total = float(deriv[i, 0]) * values[0]
                for j in range(1, 8):
                    total = total + float(deriv[i, j]) * values[j]
                volume_ref[field, i * 64 + 8 * b : i * 64 + 8 * b + 8, :] = total
        return carry

    lax.fori_loop(0, 5, body, 0)


def second_kernel(deriv, turn_ref, state_ref, before_ref, volume_ref, flux):
    axis_flux(state_ref, 1, flux)

    def body(field, carry):
        for a in range(8):
            values = [flux[field, a * 64 + 8 * b : a * 64 + 8 * b + 8, :] for b in range(8)]
            for i in range(8):
                place = slice(a * 64 + 8 * i, a * 64 + 8 * i + 8)
                total = before_ref[field, place, :]
                for j in range(8):
                    total = total + float(deriv[i, j]) * values[j]
                volume_ref[field, place, :] = total
        return carry

    lax.fori_loop(0, 5, body, 0)


def gather_kernel(split_ref, mortar_ref, face_ref, gather_ref):
    picked = jnp.dot(split_ref[...], own_choice(mortar_ref, face_ref), preferred_element_type=F32)
    gather_ref[0:ROWS, :] = thirds(picked, ROWS)
    gather_ref[ROWS : ROWS + 16, :] = picked[3 * ROWS : 3 * ROWS + 16]


def third_kernel(turn_ref, state_ref, before_ref, mix_ref, volume_ref, flux):
    axis_flux(state_ref, 2, flux)
    for half in range(2):
        part = slice(256 * half, 256 * half + 256)
        mixed = jnp.dot(
            mix_ref[...],
            jnp.concatenate([flux[field, part, :] for field in range(5)], axis=1),
            precision=HIGHEST,
            preferred_element_type=F32,
        )
        for field in range(5):
            volume_ref[field, part, :] = before_ref[field, part, :] + mixed[:, field * ELEMS : (field + 1) * ELEMS]


def trace_flux(fields, normal):
    density, one, two, three, energy = fields
    inverse = 1.0 / density
    press = (GAMMA - 1.0) * (energy - 0.5 * (one * one + two * two + three * three) * inverse)
    flow = one * normal[0] + two * normal[1] + three * normal[2]
    speed = flow * inverse
    return [
        flow,
        one * speed + press * normal[0],
        two * speed + press * normal[1],
        three * speed + press * normal[2],
        (energy + press) * speed,
    ]


def child_select(stack, index):
    lanes = slice(index * ELEMS, (index + 1) * ELEMS)
    lane = iota((64, ELEMS), 1)
    value = stack[192:256, lanes]
    for child in (2, 1, 0):
        value = jnp.where(lane < 32 * (child + 1), stack[64 * child : 64 * child + 64, lanes], value)
    return value


def by_child(matrix_ref, values):
    high, mid = split2(jnp.concatenate(values, axis=1))
    stack = jnp.dot(
        matrix_ref[...], jnp.concatenate([high, mid, high, mid], axis=0), preferred_element_type=F32
    )
    return [child_select(stack, index) for index in range(len(values))]


def face_kernel(
    devices, turn_ref, gather_ref, i0, i2, i3, i4, mortar_ref, face_ref, project_ref, back_ref,
    corr_ref, chip_ref, raw_ref, pool_ref
):
    partners = partner_of(lax.axis_index("sfc"), devices)
    incoming = gather_blocks(devices, i0, i2, i3, i4, slice(0, 384))
    remote = remote_choice(mortar_ref, face_ref, partners)
    arrived = jnp.concatenate(
        incoming + [jnp.zeros((ELEMS - PEERS * WIDTH, 384), F32)], axis=0
    ).T
    high, mid, low = split3(arrived[:ROWS])
    picked = jnp.dot(
        jnp.concatenate([high, mid, low, arrived[ROWS : ROWS + 16].astype(BF16)], axis=0),
        remote,
        preferred_element_type=F32,
    )
    pool_ref[0:ROWS, :] = gather_ref[0:ROWS, :] + thirds(picked, ROWS)
    normals = gather_ref[ROWS : ROWS + 8, :] + picked[3 * ROWS : 3 * ROWS + 8]
    sides = []
    for side in range(4):
        lanes = slice(side * ELEMS, (side + 1) * ELEMS)
        fields = [pool_ref[64 * field : 64 * field + 64, lanes] for field in range(5)]
        normal = [normals[axis : axis + 1, lanes] for axis in range(3)]
        sides.append((fields, trace_flux(fields, normal)))
    (large_u, large_f), (left_u, left_f), (child_u, child_f), (right_u, right_f) = sides
    spread = by_child(project_ref, large_u + large_f)
    steady = [0.5 * (spread[5 + k] - child_f[k]) for k in range(5)]
    moving = [0.5 * (spread[k] - child_u[k]) for k in range(5)]
    folded = by_child(back_ref, steady + moving)
    for k in range(5):
        rows = slice(64 * k, 64 * k + 64)
        more = slice(ROWS + 64 * k, ROWS + 64 * k + 64)
        corr_ref[rows, 0:128] = folded[k] - 0.25 * large_f[k]
        corr_ref[more, 0:128] = folded[5 + k]
        corr_ref[rows, 256:384] = -steady[k] - child_f[k]
        corr_ref[more, 256:384] = -moving[k]
        even = 0.5 * (left_f[k] - right_f[k])
        jump = 0.5 * (left_u[k] - right_u[k])
        corr_ref[rows, 128:256] = even - left_f[k]
        corr_ref[more, 128:256] = jump
        corr_ref[rows, 384:512] = -even - right_f[k]
        corr_ref[more, 384:512] = -jump
    back = sum(dot_nt(part, remote) for part in split3(corr_ref[...])).T
    chip_ref[...] = back[0 : 2 * WIDTH]
    raw_ref[...] = back[2 * WIDTH : 5 * WIDTH]


def reply_kernel(turn_ref, last_ref, raw_ref, chip_ref, pair_ref, next_ref, far_ref, best_ref):
    best = jnp.maximum(turn_ref[...], last_ref[...])
    best_ref[...] = best
    pair_ref[0:WIDTH, 0 : 2 * ROWS] = raw_ref[0:WIDTH, :]
    next_ref[0:WIDTH, 0 : 2 * ROWS] = raw_ref[WIDTH : 2 * WIDTH, :]
    far_ref[...] = raw_ref[2 * WIDTH : 3 * WIDTH, :]
    for ref in (pair_ref, next_ref):
        ref[WIDTH : 2 * WIDTH, 0 : 2 * ROWS] = chip_ref[WIDTH : 2 * WIDTH, :]
    for ref in (pair_ref, next_ref):
        for k in range(ref.shape[0] // 8):
            ref[8 * k : 8 * k + 8, 2 * ROWS :] = best


def lift_kernel(
    turn_ref, corr_ref, mortar_ref, face_ref, volume_ref, register_ref, scale_ref, steady_ref, rate_ref
):
    chosen = own_choice(mortar_ref, face_ref)
    scale = scale_ref[0:1, :]
    for field in range(5):
        steady_ref[field] = SECTION_A * register_ref[field]
        rate_ref[field] = -scale * volume_ref[field]
    parts = split3(corr_ref[...])
    layers = sum(dot_nt(part, chosen) for part in parts)
    lift = -LIFT * scale
    for face in range(6):
        lanes = slice(face * ELEMS, (face + 1) * ELEMS)
        for field in range(5):
            add_layer(rate_ref, field, face, lift * layers[64 * field : 64 * field + 64, lanes])
            add_layer(
                steady_ref, field, face, lift * layers[ROWS + 64 * field : ROWS + 64 * field + 64, lanes]
            )


def lift_rows(parts, lift):
    total = parts[0:64] + parts[64:128]
    return [lift * total[:, face * ELEMS : (face + 1) * ELEMS] for face in range(6)]


def finish_kernel(
    devices, steady_ref, rate_ref, state_ref, i0, i3, i4, i2, fast_ref, chosen_ref, scale_ref,
    state_hbm, register_hbm, state_out, register_out, sems
):
    fast = fast_ref[...]
    for ref in (i2, i3):
        fast = jnp.maximum(fast, ref[0:8, 2 * ROWS :])
    fast = jnp.where(iota((8, ELEMS), 1) < 80, 0.0, fast)
    lam = jnp.max(jnp.max(fast, axis=0, keepdims=True), axis=1, keepdims=True)
    inverse = 1.0 / lam
    lift = -LIFT * scale_ref[0:1, :] * inverse
    chosen = chosen_ref[...]
    arrived = jnp.concatenate(
        [
            block[:, 0:ROWS] + lam * block[:, ROWS : 2 * ROWS]
            for block in gather_blocks(devices, i0, i2, i3, i4, slice(0, 2 * ROWS))
        ]
        + [jnp.zeros((ELEMS - PEERS * WIDTH, ROWS), F32)],
        axis=0,
    ).T
    high, mid = split2(arrived)
    copies = []
    for field in range(5):
        rows = slice(64 * field, 64 * field + 64)
        parts = jnp.dot(jnp.concatenate([high[rows], mid[rows]], axis=0), chosen, preferred_element_type=F32)
        layers = lift_rows(parts, lift)
        register_out[field] = steady_ref[field] + inverse * rate_ref[field]
        for face in range(6):
            add_layer(register_out, field, face, layers[face])
        copies.append(pltpu.make_async_copy(register_out.at[field], register_hbm.at[field], sems.at[2 * field]))
        copies[-1].start()
        state_out[field] = state_ref[field] + SECTION_B * register_out[field]
        copies.append(pltpu.make_async_copy(state_out.at[field], state_hbm.at[field], sems.at[2 * field + 1]))
        copies[-1].start()
    for copy in copies:
        copy.wait()


VMEM = pl.BlockSpec(memory_space=pltpu.VMEM)
HBM = pl.BlockSpec(memory_space=pltpu.HBM)


def call(kernel, name, outs, specs, cost, scratch=(), out_specs=None):
    return pl.pallas_call(
        kernel,
        name=name,
        out_shape=[jax.ShapeDtypeStruct(shape, dtype) for shape, dtype in outs],
        in_specs=specs,
        out_specs=out_specs or [VMEM] * len(outs),
        scratch_shapes=list(scratch),
        compiler_params=pltpu.CompilerParams(vmem_limit_bytes=40 * 1024 * 1024),
        cost_estimate=pl.CostEstimate(flops=cost[0], bytes_accessed=cost[1], transcendentals=0),
    )


def per_device(state, register, metric, counts, send_slots, mortar_refs, face_refs):
    devices = lax.axis_size("sfc")
    deriv, project, back, mix = node_tables()
    metric = metric.reshape(1, ELEMS)
    sends, mortars, faces = send_slots.T, mortar_refs.T, face_refs.T
    pairs = pairings(devices)
    cube = (5, 512, ELEMS)
    flux = [pltpu.VMEM(cube, F32)]

    def exchange(value, name):
        return lax.ppermute(value, "sfc", pairs[name])

    one, two, three = [((k * WIDTH, 384), F32) for k in (1, 2, 3)]
    row = ((8, ELEMS), F32)
    split, speed = call(
        table_kernel, "table", [((3 * ROWS + 16, SLOTS), BF16), row], [VMEM], (100_000_000, 3_000_000)
    )(state)
    chip, raw, fast, scale, chosen = call(
        functools.partial(send_kernel, devices), "send", [two, three, row, row, ((ELEMS, SLOTS), BF16)], [VMEM] * 5,
        (200_000_000, 2_000_000),
    )(split, speed, counts.reshape(1, 1), sends, metric)
    chip = exchange(chip, "chip")
    onward, far, fast = call(relay_kernel, "relay", [two, one, row], [VMEM] * 3, (0, 200_000))(raw, chip, fast)
    far = exchange(far, "far")
    onward = exchange(onward, "next")
    (gathered,) = call(
        gather_kernel, "gather", [((ROWS + 16, 512), F32)], [VMEM] * 3, (1_000_000_000, 2_000_000)
    )(split, mortars, faces)
    pair, fast = call(pair_kernel, "pair", [two, row], [VMEM] * 5, (0, 200_000))(gathered, raw, chip, far, fast)
    pair = exchange(pair, "pair")
    fast = jnp.maximum(fast, pair[0:8, 256:384])
    came = exchange(fast, "y_first")
    (volume,) = call(
        functools.partial(first_kernel, deriv), "volume_first", [(cube, F32)], [VMEM] * 2,
        (1_000_000_000, 2_600_000), flux,
    )(fast, state)
    fast = jnp.maximum(fast, came)
    came = exchange(fast, "y_second")
    corrections, chip, raw = call(
        functools.partial(face_kernel, devices), "faces",
        [((2 * ROWS, 512), F32), ((2 * WIDTH, 2 * ROWS), F32), ((3 * WIDTH, 2 * ROWS), F32)],
        [VMEM] * 10, (1_000_000_000, 3_000_000), [pltpu.VMEM((ROWS, 512), F32)],
    )(fast, gathered, chip, pair, onward, far, mortars, faces, stack_terms(project), stack_terms(back))
    fast = jnp.maximum(fast, came)
    came = exchange(fast, "z_first")
    chip = exchange(chip, "chip")
    (volume,) = call(
        functools.partial(second_kernel, deriv), "volume_second", [(cube, F32)], [VMEM] * 3,
        (1_000_000_000, 3_900_000), flux,
    )(fast, state, volume)
    wide = 2 * ROWS + ELEMS
    pair, onward, far, fast = call(
        reply_kernel, "reply",
        [((2 * WIDTH, wide), F32)] * 2 + [((WIDTH, 2 * ROWS), F32), row], [VMEM] * 4, (0, 500_000),
    )(fast, came, raw, chip)
    onward = exchange(onward, "next")
    far = exchange(far, "far")
    pair = exchange(pair, "pair")
    (volume,) = call(
        third_kernel, "volume_third", [(cube, F32)], [VMEM] * 4, (1_000_000_000, 6_000_000), flux,
    )(fast, state, volume, jnp.asarray(mix))
    steady, rate = call(
        lift_kernel, "lift", [(cube, F32)] * 2, [VMEM] * 7, (1_500_000_000, 6_000_000)
    )(fast, corrections, mortars, faces, volume, register, scale)
    return tuple(
        call(
            functools.partial(finish_kernel, devices), "finish", [(cube, F32)] * 2,
            [VMEM] * 10, (200_000_000, 6_000_000),
            [pltpu.VMEM(cube, F32)] * 2 + [pltpu.SemaphoreType.DMA((10,))], [HBM] * 2,
        )(steady, rate, state, chip, onward, far, pair, fast, chosen, scale)
    )


def solution(mesh):
    return jax.shard_map(
        per_device,
        mesh=mesh,
        in_specs=(
            P(None, None, "sfc"),
            P(None, None, "sfc"),
            P("sfc"),
            P("sfc"),
            P("sfc", None),
            P("sfc", None),
            P("sfc", None),
        ),
        out_specs=(P(None, None, "sfc"), P(None, None, "sfc")),
        check_vma=False,
    )
```

```python
import functools
import jax
import jax.numpy as jnp
import numpy as np
from jax import lax
from jax.experimental import pallas as pl
from jax.experimental.pallas import tpu as pltpu
from jax.sharding import PartitionSpec as P

GAMMA = 1.4
LIFT = 28.0
COURANT = 0.02
SECTION_A = -0.4178904745
SECTION_B = 0.3792103129999
HIGHEST = lax.Precision.HIGHEST
F32 = jnp.float32
BF16 = jnp.bfloat16
ELEMS = 128
SLOTS = 6 * ELEMS
WIDTH = 16
PEERS = 5
MORTARS = 32
FACES = 128
ROWS = 320
GLL_NODES = (
    -1.0,
    -0.8717401485096066,
    -0.5917001814331423,
    -0.2092992179024789,
    0.2092992179024789,
    0.5917001814331423,
    0.8717401485096066,
    1.0,
)
GLL_WEIGHTS = (
    0.03571428571428571,
    0.2107042271435061,
    0.3411226924835044,
    0.4124587946587038,
    0.4124587946587038,
    0.3411226924835044,
    0.2107042271435061,
    0.03571428571428571,
)


def interp_matrix(nodes, points):
    matrix = np.ones((len(points), len(nodes)))
    for source in range(len(nodes)):
        for other in range(len(nodes)):
            if other != source:
                matrix[:, source] *= (points - nodes[other]) / (nodes[source] - nodes[other])
    return matrix


def node_tables():
    number = 8
    nodes = np.array(GLL_NODES)
    weights = np.array(GLL_WEIGHTS)
    differ = nodes[:, None] - nodes[None, :] + np.eye(number)
    barycentric = 1.0 / np.prod(differ, axis=1)
    deriv = barycentric[None, :] / barycentric[:, None] / differ
    deriv = deriv * (1.0 - np.eye(number))
    deriv = deriv - np.eye(number) * deriv.sum(axis=1)[:, None]
    halves = [interp_matrix(nodes, (nodes - 1.0) / 2.0), interp_matrix(nodes, (nodes + 1.0) / 2.0)]
    backs = [0.5 * (half.T * weights[None, :]) / weights[:, None] for half in halves]
    project = np.concatenate([np.kron(halves[c // 2], halves[c % 2]) for c in range(4)], axis=0)
    back = np.concatenate([np.kron(backs[c // 2], backs[c % 2]) for c in range(4)], axis=0)
    return (
        deriv.astype(np.float32),
        project.astype(np.float32),
        back.astype(np.float32),
        np.kron(np.eye(32), deriv).astype(np.float32),
    )


def pairings(devices):
    index = np.arange(devices)
    low = index % 4 < 2
    y = index // 8 % 4
    partners = dict(
        chip=index ^ 1,
        pair=np.where(low, index + 2, index - 2) % devices,
        next=np.where(low, index - 2, index + 2) % devices,
        far=(index + devices // 2) % devices,
        y_first=index ^ 9,
        y_second=(index + 8 * (np.where(y % 2 == 1, y + 1, y - 1) % 4 - y)) ^ 1,
        z_first=index ^ 33,
    )
    return {name: [(int(d), int(p)) for d, p in enumerate(side)] for name, side in partners.items()}


def partner_of(me, devices):
    odd = me % 2
    low = jnp.where(me % 4 < 2, 2, -2)
    steps = [1 - 2 * odd, 2 * odd - 1, low, -low, devices // 2]
    return [lax.rem(me + step + devices, devices) for step in steps]


def split2(value):
    high = value.astype(BF16)
    return high, (value - high.astype(F32)).astype(BF16)


def stack_terms(matrix):
    high = matrix.astype(BF16)
    mid = (matrix - high.astype(np.float32)).astype(BF16)
    return jnp.asarray(np.concatenate([high, high, mid, mid], axis=1))


def iota(shape, dim):
    return lax.broadcasted_iota(jnp.int32, shape, dim)


def dot_nt(left, right):
    return lax.dot_general(left, right, (((1,), (1,)), ((), ())), preferred_element_type=F32)


def one_hot(mask):
    return jnp.where(mask, F32(1.0), F32(0.0)).astype(BF16)


def halves(value, size):
    return value[:size] + value[size : 2 * size]


def face_layer(ref, field, face):
    axis, side = face // 2, face % 2
    if axis == 0:
        return ref[field, 448 * side : 448 * side + 64, :]
    if axis == 1:
        return jnp.concatenate(
            [ref[field, a * 64 + 56 * side : a * 64 + 56 * side + 8, :] for a in range(8)], axis=0
        )
    return ref[field, pl.ds(7 * side, 64, stride=8), :]


def add_layer(ref, field, face, value):
    axis, side = face // 2, face % 2
    if axis == 0:
        ref[field, 448 * side : 448 * side + 64, :] += value
    elif axis == 1:
        for a in range(8):
            ref[field, a * 64 + 56 * side : a * 64 + 56 * side + 8, :] += value[8 * a : 8 * a + 8]
    else:
        place = pl.ds(7 * side, 64, stride=8)
        ref[field, place, :] = ref[field, place, :] + value


def out_columns(slots_ref, partners):
    lane = iota((WIDTH, ELEMS), 1)
    slots = slots_ref[...]
    columns = [
        jnp.sum(jnp.where(lane == partners[peer], slots, 0), axis=1, keepdims=True) for peer in range(PEERS)
    ]
    columns.append(jnp.full((ELEMS - PEERS * WIDTH, 1), SLOTS, jnp.int32))
    return jnp.concatenate(columns, axis=0)


def ref_rows(mortar_ref, face_ref):
    large = mortar_ref[0:1, :]
    return jnp.concatenate(
        [large] * 4 + [face_ref[0:1, :]] + [mortar_ref[c : c + 1, :] for c in range(1, 5)] + [face_ref[1:2, :]],
        axis=1,
    )


def own_choice(mortar_ref, face_ref):
    return one_hot(ref_rows(mortar_ref, face_ref) == iota((SLOTS, 512), 0))


def remote_choice(mortar_ref, face_ref, partners):
    place = iota((ELEMS, 1), 0)
    target = jnp.full((ELEMS, 1), -1, jnp.int32)
    for peer in range(PEERS):
        inside = (place >= peer * WIDTH) & (place < (peer + 1) * WIDTH)
        target = jnp.where(inside, SLOTS + partners[peer] * WIDTH + place - peer * WIDTH, target)
    return one_hot(ref_rows(mortar_ref, face_ref) == target)


def table_kernel(state_ref, split_ref, speed_ref):
    fastest = jnp.zeros((8, ELEMS), F32)
    for a in range(8):
        part = slice(64 * a, 64 * a + 64)
        density, one, two, three, energy = [state_ref[field, part, :] for field in range(5)]
        inverse = 1.0 / density
        square = one * one + two * two + three * three
        press = (GAMMA - 1.0) * (energy - 0.5 * square * inverse)
        speed = jnp.sqrt(square) * inverse + jnp.sqrt(GAMMA * press * inverse)
        fastest = jnp.maximum(fastest, jnp.max(speed.reshape(8, 8, ELEMS), axis=0))
    speed_ref[...] = fastest
    for face in range(6):
        lanes = slice(face * ELEMS, (face + 1) * ELEMS)
        for field in range(5):
            parts = split2(face_layer(state_ref, field, face))
            for term in range(2):
                split_ref[term * ROWS + field * 64 : term * ROWS + field * 64 + 64, lanes] = parts[term]
    row = iota((16, SLOTS), 0)
    face = iota((16, SLOTS), 1) // ELEMS
    sign = jnp.where(face % 2 == 1, F32(1.0), F32(-1.0))
    split_ref[2 * ROWS : 2 * ROWS + 16, :] = jnp.where(row == face // 2, sign, 0.0).astype(BF16)


def send_kernel(
    devices, split_ref, speed_ref, count_ref, slots_ref, metric_ref, chip_ref, raw_ref, fast_ref, scale_ref, chosen_ref
):
    partners = partner_of(lax.axis_index("sfc"), devices)
    live = iota((8, ELEMS), 1) < count_ref[...]
    scale_ref[...] = jnp.where(live, COURANT * metric_ref[...], 0.0)
    fastest = jnp.max(jnp.where(live, speed_ref[...], 0.0), axis=0, keepdims=True)
    fastest = jnp.max(fastest, axis=1, keepdims=True)
    fast_ref[...] = jnp.broadcast_to(fastest, (8, ELEMS))
    chosen = one_hot(out_columns(slots_ref, partners) == iota((ELEMS, SLOTS), 1))
    chosen_ref[...] = chosen
    picked = dot_nt(split_ref[...], chosen)
    rows = jnp.concatenate(
        [halves(picked, ROWS), picked[2 * ROWS : 2 * ROWS + 16], jnp.broadcast_to(fastest, (48, ELEMS))], axis=0
    )
    message = rows.T
    chip_ref[...] = message[0 : 2 * WIDTH]
    raw_ref[...] = message[2 * WIDTH : 5 * WIDTH]


def relay_kernel(raw_ref, chip_ref, fast_ref, next_ref, far_ref, best_ref):
    best = jnp.maximum(fast_ref[...], chip_ref[0:8, 256:384])
    best_ref[...] = best
    next_ref[0:WIDTH, :] = raw_ref[WIDTH : 2 * WIDTH, :]
    next_ref[WIDTH : 2 * WIDTH, :] = chip_ref[WIDTH : 2 * WIDTH, :]
    far_ref[...] = raw_ref[2 * WIDTH : 3 * WIDTH, :]
    far_ref[0:8, 256:384] = jnp.where(iota((8, ELEMS), 1) < 80, raw_ref[2 * WIDTH : 2 * WIDTH + 8, 256:384], best)


def pair_kernel(turn_ref, raw_ref, chip_ref, far_ref, fast_ref, pair_ref, best_ref):
    best = jnp.maximum(fast_ref[...], far_ref[0:8, 256:384])
    best_ref[...] = best
    pair_ref[0:WIDTH, :] = raw_ref[0:WIDTH, :]
    pair_ref[WIDTH : 2 * WIDTH, :] = chip_ref[WIDTH : 2 * WIDTH, :]
    pair_ref[0:8, 256:384] = jnp.where(iota((8, ELEMS), 1) < 80, raw_ref[0:8, 256:384], best)


def gather_blocks(devices, chip_ref, pair_ref, next_ref, far_ref, columns):
    place = lax.axis_index("sfc") % 4
    first = slice(0, WIDTH)
    second = slice(WIDTH, 2 * WIDTH)
    passed = jnp.where((place == 0) | (place == 3), next_ref[second, columns], pair_ref[second, columns])
    return [chip_ref[first, columns], passed, pair_ref[first, columns], next_ref[first, columns], far_ref[first, columns]]


def axis_flux(state_ref, axis, ref):
    for a in range(8):
        part = slice(64 * a, 64 * a + 64)
        density, one, two, three, energy = [state_ref[field, part, :] for field in range(5)]
        inverse = 1.0 / density
        press = (GAMMA - 1.0) * (energy - 0.5 * (one * one + two * two + three * three) * inverse)
        flow = (one, two, three)[axis]
        speed = flow * inverse
        terms = [one * speed, two * speed, three * speed]
        terms[axis] = terms[axis] + press
        for field, value in enumerate([flow] + terms + [(energy + press) * speed]):
            ref[field, part, :] = value


def first_kernel(deriv, turn_ref, state_ref, volume_ref, flux):
    axis_flux(state_ref, 0, flux)

    def body(field, carry):
        for b in range(8):
            values = [flux[field, a * 64 + 8 * b : a * 64 + 8 * b + 8, :] for a in range(8)]
            for i in range(8):
                total = float(deriv[i, 0]) * values[0]
                for j in range(1, 8):
                    total = total + float(deriv[i, j]) * values[j]
                volume_ref[field, i * 64 + 8 * b : i * 64 + 8 * b + 8, :] = total
        return carry

    lax.fori_loop(0, 5, body, 0)


def second_kernel(deriv, turn_ref, state_ref, before_ref, volume_ref, flux):
    axis_flux(state_ref, 1, flux)

    def body(field, carry):
        for a in range(8):
            values = [flux[field, a * 64 + 8 * b : a * 64 + 8 * b + 8, :] for b in range(8)]
            for i in range(8):
                place = slice(a * 64 + 8 * i, a * 64 + 8 * i + 8)
                total = before_ref[field, place, :]
                for j in range(8):
                    total = total + float(deriv[i, j]) * values[j]
                volume_ref[field, place, :] = total
        return carry

    lax.fori_loop(0, 5, body, 0)


def gather_kernel(split_ref, mortar_ref, face_ref, gather_ref):
    picked = jnp.dot(split_ref[...], own_choice(mortar_ref, face_ref), preferred_element_type=F32)
    gather_ref[0:ROWS, :] = halves(picked, ROWS)
    gather_ref[ROWS : ROWS + 16, :] = picked[2 * ROWS : 2 * ROWS + 16]


def third_kernel(turn_ref, state_ref, before_ref, mix_ref, volume_ref, flux):
    axis_flux(state_ref, 2, flux)
    for half in range(2):
        part = slice(256 * half, 256 * half + 256)
        mixed = jnp.dot(
            mix_ref[...],
            jnp.concatenate([flux[field, part, :] for field in range(5)], axis=1),
            precision=HIGHEST,
            preferred_element_type=F32,
        )
        for field in range(5):
            volume_ref[field, part, :] = before_ref[field, part, :] + mixed[:, field * ELEMS : (field + 1) * ELEMS]


def trace_flux(fields, normal):
    density, one, two, three, energy = fields
    inverse = 1.0 / density
    press = (GAMMA - 1.0) * (energy - 0.5 * (one * one + two * two + three * three) * inverse)
    flow = one * normal[0] + two * normal[1] + three * normal[2]
    speed = flow * inverse
    return [
        flow,
        one * speed + press * normal[0],
        two * speed + press * normal[1],
        three * speed + press * normal[2],
        (energy + press) * speed,
    ]


def child_select(stack, index):
    lanes = slice(index * ELEMS, (index + 1) * ELEMS)
    lane = iota((64, ELEMS), 1)
    value = stack[192:256, lanes]
    for child in (2, 1, 0):
        value = jnp.where(lane < 32 * (child + 1), stack[64 * child : 64 * child + 64, lanes], value)
    return value


def by_child(matrix_ref, values):
    high, mid = split2(jnp.concatenate(values, axis=1))
    stack = jnp.dot(
        matrix_ref[...], jnp.concatenate([high, mid, high, mid], axis=0), preferred_element_type=F32
    )
    return [child_select(stack, index) for index in range(len(values))]


def face_kernel(
    devices, turn_ref, gather_ref, i0, i2, i3, i4, mortar_ref, face_ref, project_ref, back_ref,
    corr_ref, chip_ref, raw_ref, pool_ref
):
    partners = partner_of(lax.axis_index("sfc"), devices)
    incoming = gather_blocks(devices, i0, i2, i3, i4, slice(0, 384))
    remote = remote_choice(mortar_ref, face_ref, partners)
    arrived = jnp.concatenate(
        incoming + [jnp.zeros((ELEMS - PEERS * WIDTH, 384), F32)], axis=0
    ).T
    high, mid = split2(arrived[:ROWS])
    picked = jnp.dot(
        jnp.concatenate([high, mid, arrived[ROWS : ROWS + 16].astype(BF16)], axis=0),
        remote,
        preferred_element_type=F32,
    )
    pool_ref[0:ROWS, :] = gather_ref[0:ROWS, :] + halves(picked, ROWS)
    normals = gather_ref[ROWS : ROWS + 8, :] + picked[2 * ROWS : 2 * ROWS + 8]
    sides = []
    for side in range(4):
        lanes = slice(side * ELEMS, (side + 1) * ELEMS)
        fields = [pool_ref[64 * field : 64 * field + 64, lanes] for field in range(5)]
        normal = [normals[axis : axis + 1, lanes] for axis in range(3)]
        sides.append((fields, trace_flux(fields, normal)))
    (large_u, large_f), (left_u, left_f), (child_u, child_f), (right_u, right_f) = sides
    spread = by_child(project_ref, large_u + large_f)
    steady = [0.5 * (spread[5 + k] - child_f[k]) for k in range(5)]
    moving = [0.5 * (spread[k] - child_u[k]) for k in range(5)]
    folded = by_child(back_ref, steady + moving)
    for k in range(5):
        rows = slice(64 * k, 64 * k + 64)
        more = slice(ROWS + 64 * k, ROWS + 64 * k + 64)
        corr_ref[rows, 0:128] = folded[k] - 0.25 * large_f[k]
        corr_ref[more, 0:128] = folded[5 + k]
        corr_ref[rows, 256:384] = -steady[k] - child_f[k]
        corr_ref[more, 256:384] = -moving[k]
        even = 0.5 * (left_f[k] - right_f[k])
        jump = 0.5 * (left_u[k] - right_u[k])
        corr_ref[rows, 128:256] = even - left_f[k]
        corr_ref[more, 128:256] = jump
        corr_ref[rows, 384:512] = -even - right_f[k]
        corr_ref[more, 384:512] = -jump
    back = sum(dot_nt(part, remote) for part in split2(corr_ref[...])).T
    chip_ref[...] = back[0 : 2 * WIDTH]
    raw_ref[...] = back[2 * WIDTH : 5 * WIDTH]


def reply_kernel(turn_ref, last_ref, raw_ref, chip_ref, pair_ref, next_ref, far_ref, best_ref):
    best = jnp.maximum(turn_ref[...], last_ref[...])
    best_ref[...] = best
    pair_ref[0:WIDTH, 0 : 2 * ROWS] = raw_ref[0:WIDTH, :]
    next_ref[0:WIDTH, 0 : 2 * ROWS] = raw_ref[WIDTH : 2 * WIDTH, :]
    far_ref[...] = raw_ref[2 * WIDTH : 3 * WIDTH, :]
    for ref in (pair_ref, next_ref):
        ref[WIDTH : 2 * WIDTH, 0 : 2 * ROWS] = chip_ref[WIDTH : 2 * WIDTH, :]
    for ref in (pair_ref, next_ref):
        for k in range(ref.shape[0] // 8):
            ref[8 * k : 8 * k + 8, 2 * ROWS :] = best


def lift_kernel(
    turn_ref, corr_ref, mortar_ref, face_ref, volume_ref, register_ref, scale_ref, steady_ref, rate_ref
):
    chosen = own_choice(mortar_ref, face_ref)
    scale = scale_ref[0:1, :]
    for field in range(5):
        steady_ref[field] = SECTION_A * register_ref[field]
        rate_ref[field] = -scale * volume_ref[field]
    parts = split2(corr_ref[...])
    layers = sum(dot_nt(part, chosen) for part in parts)
    lift = -LIFT * scale
    for face in range(6):
        lanes = slice(face * ELEMS, (face + 1) * ELEMS)
        for field in range(5):
            add_layer(rate_ref, field, face, lift * layers[64 * field : 64 * field + 64, lanes])
            add_layer(
                steady_ref, field, face, lift * layers[ROWS + 64 * field : ROWS + 64 * field + 64, lanes]
            )


def lift_rows(parts, lift):
    total = parts[0:64] + parts[64:128]
    return [lift * total[:, face * ELEMS : (face + 1) * ELEMS] for face in range(6)]


def finish_kernel(
    devices, steady_ref, rate_ref, state_ref, i0, i3, i4, i2, fast_ref, chosen_ref, scale_ref,
    state_hbm, register_hbm, state_out, register_out, sems
):
    fast = fast_ref[...]
    for ref in (i2, i3):
        fast = jnp.maximum(fast, ref[0:8, 2 * ROWS :])
    fast = jnp.where(iota((8, ELEMS), 1) < 80, 0.0, fast)
    lam = jnp.max(jnp.max(fast, axis=0, keepdims=True), axis=1, keepdims=True)
    inverse = 1.0 / lam
    lift = -LIFT * scale_ref[0:1, :] * inverse
    chosen = chosen_ref[...]
    arrived = jnp.concatenate(
        [
            block[:, 0:ROWS] + lam * block[:, ROWS : 2 * ROWS]
            for block in gather_blocks(devices, i0, i2, i3, i4, slice(0, 2 * ROWS))
        ]
        + [jnp.zeros((ELEMS - PEERS * WIDTH, ROWS), F32)],
        axis=0,
    ).T
    high, mid = split2(arrived)
    copies = []
    for field in range(5):
        rows = slice(64 * field, 64 * field + 64)
        parts = jnp.dot(jnp.concatenate([high[rows], mid[rows]], axis=0), chosen, preferred_element_type=F32)
        layers = lift_rows(parts, lift)
        register_out[field] = steady_ref[field] + inverse * rate_ref[field]
        for face in range(6):
            add_layer(register_out, field, face, layers[face])
        copies.append(pltpu.make_async_copy(register_out.at[field], register_hbm.at[field], sems.at[2 * field]))
        copies[-1].start()
        state_out[field] = state_ref[field] + SECTION_B * register_out[field]
        copies.append(pltpu.make_async_copy(state_out.at[field], state_hbm.at[field], sems.at[2 * field + 1]))
        copies[-1].start()
    for copy in copies:
        copy.wait()


VMEM = pl.BlockSpec(memory_space=pltpu.VMEM)
HBM = pl.BlockSpec(memory_space=pltpu.HBM)


def call(kernel, name, outs, specs, cost, scratch=(), out_specs=None):
    return pl.pallas_call(
        kernel,
        name=name,
        out_shape=[jax.ShapeDtypeStruct(shape, dtype) for shape, dtype in outs],
        in_specs=specs,
        out_specs=out_specs or [VMEM] * len(outs),
        scratch_shapes=list(scratch),
        compiler_params=pltpu.CompilerParams(vmem_limit_bytes=40 * 1024 * 1024),
        cost_estimate=pl.CostEstimate(flops=cost[0], bytes_accessed=cost[1], transcendentals=0),
    )


def per_device(state, register, metric, counts, send_slots, mortar_refs, face_refs):
    devices = lax.axis_size("sfc")
    deriv, project, back, mix = node_tables()
    metric = metric.reshape(1, ELEMS)
    sends, mortars, faces = send_slots.T, mortar_refs.T, face_refs.T
    pairs = pairings(devices)
    cube = (5, 512, ELEMS)
    flux = [pltpu.VMEM(cube, F32)]

    def exchange(value, name):
        return lax.ppermute(value, "sfc", pairs[name])

    one, two, three = [((k * WIDTH, 384), F32) for k in (1, 2, 3)]
    row = ((8, ELEMS), F32)
    split, speed = call(
        table_kernel, "table", [((2 * ROWS + 16, SLOTS), BF16), row], [VMEM], (100_000_000, 3_000_000)
    )(state)
    chip, raw, fast, scale, chosen = call(
        functools.partial(send_kernel, devices), "send", [two, three, row, row, ((ELEMS, SLOTS), BF16)], [VMEM] * 5,
        (200_000_000, 2_000_000),
    )(split, speed, counts.reshape(1, 1), sends, metric)
    chip = exchange(chip, "chip")
    onward, far, fast = call(relay_kernel, "relay", [two, one, row], [VMEM] * 3, (0, 200_000))(raw, chip, fast)
    far = exchange(far, "far")
    onward = exchange(onward, "next")
    (gathered,) = call(
        gather_kernel, "gather", [((ROWS + 16, 512), F32)], [VMEM] * 3, (1_000_000_000, 2_000_000)
    )(split, mortars, faces)
    pair, fast = call(pair_kernel, "pair", [two, row], [VMEM] * 5, (0, 200_000))(gathered, raw, chip, far, fast)
    pair = exchange(pair, "pair")
    fast = jnp.maximum(fast, pair[0:8, 256:384])
    came = exchange(fast, "y_first")
    (volume,) = call(
        functools.partial(first_kernel, deriv), "volume_first", [(cube, F32)], [VMEM] * 2,
        (1_000_000_000, 2_600_000), flux,
    )(fast, state)
    fast = jnp.maximum(fast, came)
    came = exchange(fast, "y_second")
    corrections, chip, raw = call(
        functools.partial(face_kernel, devices), "faces",
        [((2 * ROWS, 512), F32), ((2 * WIDTH, 2 * ROWS), F32), ((3 * WIDTH, 2 * ROWS), F32)],
        [VMEM] * 10, (1_000_000_000, 3_000_000), [pltpu.VMEM((ROWS, 512), F32)],
    )(fast, gathered, chip, pair, onward, far, mortars, faces, stack_terms(project), stack_terms(back))
    fast = jnp.maximum(fast, came)
    came = exchange(fast, "z_first")
    chip = exchange(chip, "chip")
    (volume,) = call(
        functools.partial(second_kernel, deriv), "volume_second", [(cube, F32)], [VMEM] * 3,
        (1_000_000_000, 3_900_000), flux,
    )(fast, state, volume)
    wide = 2 * ROWS + ELEMS
    pair, onward, far, fast = call(
        reply_kernel, "reply",
        [((2 * WIDTH, wide), F32)] * 2 + [((WIDTH, 2 * ROWS), F32), row], [VMEM] * 4, (0, 500_000),
    )(fast, came, raw, chip)
    onward = exchange(onward, "next")
    far = exchange(far, "far")
    pair = exchange(pair, "pair")
    (volume,) = call(
        third_kernel, "volume_third", [(cube, F32)], [VMEM] * 4, (1_000_000_000, 6_000_000), flux,
    )(fast, state, volume, jnp.asarray(mix))
    steady, rate = call(
        lift_kernel, "lift", [(cube, F32)] * 2, [VMEM] * 7, (1_500_000_000, 6_000_000)
    )(fast, corrections, mortars, faces, volume, register, scale)
    return tuple(
        call(
            functools.partial(finish_kernel, devices), "finish", [(cube, F32)] * 2,
            [VMEM] * 10, (200_000_000, 6_000_000),
            [pltpu.VMEM(cube, F32)] * 2 + [pltpu.SemaphoreType.DMA((10,))], [HBM] * 2,
        )(steady, rate, state, chip, onward, far, pair, fast, chosen, scale)
    )


def solution(mesh):
    return jax.shard_map(
        per_device,
        mesh=mesh,
        in_specs=(
            P(None, None, "sfc"),
            P(None, None, "sfc"),
            P("sfc"),
            P("sfc"),
            P("sfc", None),
            P("sfc", None),
            P("sfc", None),
        ),
        out_specs=(P(None, None, "sfc"), P(None, None, "sfc")),
        check_vma=False,
    )
```

```python
import functools
import jax
import jax.numpy as jnp
import numpy as np
from jax import lax
from jax.experimental import pallas as pl
from jax.experimental.pallas import tpu as pltpu
from jax.sharding import PartitionSpec as P

GAMMA = 1.4
LIFT = 28.0
COURANT = 0.02
SECTION_A = -0.4178904745
SECTION_B = 0.3792103129999
HIGHEST = lax.Precision.HIGHEST
F32 = jnp.float32
BF16 = jnp.bfloat16
ELEMS = 128
SLOTS = 6 * ELEMS
WIDTH = 16
PEERS = 5
MORTARS = 32
FACES = 128
ROWS = 320
GLL_NODES = (
    -1.0,
    -0.8717401485096066,
    -0.5917001814331423,
    -0.2092992179024789,
    0.2092992179024789,
    0.5917001814331423,
    0.8717401485096066,
    1.0,
)
GLL_WEIGHTS = (
    0.03571428571428571,
    0.2107042271435061,
    0.3411226924835044,
    0.4124587946587038,
    0.4124587946587038,
    0.3411226924835044,
    0.2107042271435061,
    0.03571428571428571,
)


def interp_matrix(nodes, points):
    matrix = np.ones((len(points), len(nodes)))
    for source in range(len(nodes)):
        for other in range(len(nodes)):
            if other != source:
                matrix[:, source] *= (points - nodes[other]) / (nodes[source] - nodes[other])
    return matrix


def node_tables():
    number = 8
    nodes = np.array(GLL_NODES)
    weights = np.array(GLL_WEIGHTS)
    differ = nodes[:, None] - nodes[None, :] + np.eye(number)
    barycentric = 1.0 / np.prod(differ, axis=1)
    deriv = barycentric[None, :] / barycentric[:, None] / differ
    deriv = deriv * (1.0 - np.eye(number))
    deriv = deriv - np.eye(number) * deriv.sum(axis=1)[:, None]
    halves = [interp_matrix(nodes, (nodes - 1.0) / 2.0), interp_matrix(nodes, (nodes + 1.0) / 2.0)]
    backs = [0.5 * (half.T * weights[None, :]) / weights[:, None] for half in halves]
    project = np.concatenate([np.kron(halves[c // 2], halves[c % 2]) for c in range(4)], axis=0)
    back = np.concatenate([np.kron(backs[c // 2], backs[c % 2]) for c in range(4)], axis=0)
    return (
        deriv.astype(np.float32),
        project.astype(np.float32),
        back.astype(np.float32),
        np.kron(np.eye(32), deriv).astype(np.float32),
    )


def pairings(devices):
    index = np.arange(devices)
    low = index % 4 < 2
    y = index // 8 % 4
    partners = dict(
        chip=index ^ 1,
        pair=np.where(low, index + 2, index - 2) % devices,
        next=np.where(low, index - 2, index + 2) % devices,
        far=(index + devices // 2) % devices,
        y_first=index ^ 9,
        y_second=(index + 8 * (np.where(y % 2 == 1, y + 1, y - 1) % 4 - y)) ^ 1,
        z_first=index ^ 33,
    )
    return {name: [(int(d), int(p)) for d, p in enumerate(side)] for name, side in partners.items()}


def partner_of(me, devices):
    odd = me % 2
    low = jnp.where(me % 4 < 2, 2, -2)
    steps = [1 - 2 * odd, 2 * odd - 1, low, -low, devices // 2]
    return [lax.rem(me + step + devices, devices) for step in steps]


def split2(value):
    high = value.astype(BF16)
    return high, (value - high.astype(F32)).astype(BF16)


def stack_terms(matrix):
    high = matrix.astype(BF16)
    mid = (matrix - high.astype(np.float32)).astype(BF16)
    return jnp.asarray(np.concatenate([high, high, mid, mid], axis=1))


def iota(shape, dim):
    return lax.broadcasted_iota(jnp.int32, shape, dim)


def dot_nt(left, right):
    return lax.dot_general(left, right, (((1,), (1,)), ((), ())), preferred_element_type=F32)


def one_hot(mask):
    return jnp.where(mask, F32(1.0), F32(0.0)).astype(BF16)


def halves(value, size):
    return value[:size] + value[size : 2 * size]


def face_layer(ref, field, face):
    axis, side = face // 2, face % 2
    if axis == 0:
        return ref[field, 448 * side : 448 * side + 64, :]
    if axis == 1:
        return jnp.concatenate(
            [ref[field, a * 64 + 56 * side : a * 64 + 56 * side + 8, :] for a in range(8)], axis=0
        )
    return ref[field, pl.ds(7 * side, 64, stride=8), :]


def add_layer(ref, field, face, value):
    axis, side = face // 2, face % 2
    if axis == 0:
        ref[field, 448 * side : 448 * side + 64, :] += value
    elif axis == 1:
        for a in range(8):
            ref[field, a * 64 + 56 * side : a * 64 + 56 * side + 8, :] += value[8 * a : 8 * a + 8]
    else:
        place = pl.ds(7 * side, 64, stride=8)
        ref[field, place, :] = ref[field, place, :] + value


def out_columns(slots_ref, partners):
    lane = iota((WIDTH, ELEMS), 1)
    slots = slots_ref[...]
    columns = [
        jnp.sum(jnp.where(lane == partners[peer], slots, 0), axis=1, keepdims=True) for peer in range(PEERS)
    ]
    columns.append(jnp.full((ELEMS - PEERS * WIDTH, 1), SLOTS, jnp.int32))
    return jnp.concatenate(columns, axis=0)


def ref_rows(mortar_ref, face_ref):
    large = mortar_ref[0:1, :]
    return jnp.concatenate(
        [large] * 4 + [face_ref[0:1, :]] + [mortar_ref[c : c + 1, :] for c in range(1, 5)] + [face_ref[1:2, :]],
        axis=1,
    )


def own_choice(mortar_ref, face_ref):
    return one_hot(ref_rows(mortar_ref, face_ref) == iota((SLOTS, 512), 0))


def remote_choice(mortar_ref, face_ref, partners):
    place = iota((ELEMS, 1), 0)
    target = jnp.full((ELEMS, 1), -1, jnp.int32)
    for peer in range(PEERS):
        inside = (place >= peer * WIDTH) & (place < (peer + 1) * WIDTH)
        target = jnp.where(inside, SLOTS + partners[peer] * WIDTH + place - peer * WIDTH, target)
    return one_hot(ref_rows(mortar_ref, face_ref) == target)


def table_kernel(state_ref, split_ref, speed_ref):
    fastest = jnp.zeros((8, ELEMS), F32)
    for a in range(8):
        part = slice(64 * a, 64 * a + 64)
        density, one, two, three, energy = [state_ref[field, part, :] for field in range(5)]
        inverse = 1.0 / density
        square = one * one + two * two + three * three
        press = (GAMMA - 1.0) * (energy - 0.5 * square * inverse)
        speed = jnp.sqrt(square) * inverse + jnp.sqrt(GAMMA * press * inverse)
        fastest = jnp.maximum(fastest, jnp.max(speed.reshape(8, 8, ELEMS), axis=0))
    speed_ref[...] = fastest
    for face in range(6):
        lanes = slice(face * ELEMS, (face + 1) * ELEMS)
        for field in range(5):
            parts = split2(face_layer(state_ref, field, face))
            for term in range(2):
                split_ref[term * ROWS + field * 64 : term * ROWS + field * 64 + 64, lanes] = parts[term]
    row = iota((16, SLOTS), 0)
    face = iota((16, SLOTS), 1) // ELEMS
    sign = jnp.where(face % 2 == 1, F32(1.0), F32(-1.0))
    split_ref[2 * ROWS : 2 * ROWS + 16, :] = jnp.where(row == face // 2, sign, 0.0).astype(BF16)


def send_kernel(
    devices, split_ref, speed_ref, count_ref, slots_ref, metric_ref, chip_ref, raw_ref, fast_ref, scale_ref, chosen_ref
):
    partners = partner_of(lax.axis_index("sfc"), devices)
    live = iota((8, ELEMS), 1) < count_ref[...]
    scale_ref[...] = jnp.where(live, COURANT * metric_ref[...], 0.0)
    fastest = jnp.max(jnp.where(live, speed_ref[...], 0.0), axis=0, keepdims=True)
    fastest = jnp.max(fastest, axis=1, keepdims=True)
    fast_ref[...] = jnp.broadcast_to(fastest, (8, ELEMS))
    chosen = one_hot(out_columns(slots_ref, partners) == iota((ELEMS, SLOTS), 1))
    chosen_ref[...] = chosen
    picked = dot_nt(split_ref[...], chosen)
    rows = jnp.concatenate(
        [halves(picked, ROWS), picked[2 * ROWS : 2 * ROWS + 16], jnp.broadcast_to(fastest, (48, ELEMS))], axis=0
    )
    message = rows.T
    chip_ref[...] = message[0 : 2 * WIDTH]
    raw_ref[...] = message[2 * WIDTH : 5 * WIDTH]


def relay_kernel(raw_ref, chip_ref, fast_ref, next_ref, far_ref, best_ref):
    best = jnp.maximum(fast_ref[...], chip_ref[0:8, 256:384])
    best_ref[...] = best
    next_ref[0:WIDTH, :] = raw_ref[WIDTH : 2 * WIDTH, :]
    next_ref[WIDTH : 2 * WIDTH, :] = chip_ref[WIDTH : 2 * WIDTH, :]
    far_ref[...] = raw_ref[2 * WIDTH : 3 * WIDTH, :]
    far_ref[0:8, 256:384] = jnp.where(iota((8, ELEMS), 1) < 80, raw_ref[2 * WIDTH : 2 * WIDTH + 8, 256:384], best)


def pair_kernel(turn_ref, raw_ref, chip_ref, far_ref, fast_ref, pair_ref, best_ref):
    best = jnp.maximum(fast_ref[...], far_ref[0:8, 256:384])
    best_ref[...] = best
    pair_ref[0:WIDTH, :] = raw_ref[0:WIDTH, :]
    pair_ref[WIDTH : 2 * WIDTH, :] = chip_ref[WIDTH : 2 * WIDTH, :]
    pair_ref[0:8, 256:384] = jnp.where(iota((8, ELEMS), 1) < 80, raw_ref[0:8, 256:384], best)


def gather_blocks(devices, chip_ref, pair_ref, next_ref, far_ref, columns):
    place = lax.axis_index("sfc") % 4
    first = slice(0, WIDTH)
    second = slice(WIDTH, 2 * WIDTH)
    passed = jnp.where((place == 0) | (place == 3), next_ref[second, columns], pair_ref[second, columns])
    return [chip_ref[first, columns], passed, pair_ref[first, columns], next_ref[first, columns], far_ref[first, columns]]


def axis_flux(state_ref, axis, ref):
    for a in range(8):
        part = slice(64 * a, 64 * a + 64)
        density, one, two, three, energy = [state_ref[field, part, :] for field in range(5)]
        inverse = 1.0 / density
        press = (GAMMA - 1.0) * (energy - 0.5 * (one * one + two * two + three * three) * inverse)
        flow = (one, two, three)[axis]
        speed = flow * inverse
        terms = [one * speed, two * speed, three * speed]
        terms[axis] = terms[axis] + press
        for field, value in enumerate([flow] + terms + [(energy + press) * speed]):
            ref[field, part, :] = value


def first_kernel(deriv, turn_ref, state_ref, volume_ref, flux):
    axis_flux(state_ref, 0, flux)

    def body(field, carry):
        for b in range(8):
            values = [flux[field, a * 64 + 8 * b : a * 64 + 8 * b + 8, :] for a in range(8)]
            for i in range(8):
                total = float(deriv[i, 0]) * values[0]
                for j in range(1, 8):
                    total = total + float(deriv[i, j]) * values[j]
                volume_ref[field, i * 64 + 8 * b : i * 64 + 8 * b + 8, :] = total
        return carry

    lax.fori_loop(0, 5, body, 0)


def second_kernel(deriv, turn_ref, state_ref, before_ref, volume_ref, flux):
    axis_flux(state_ref, 1, flux)

    def body(field, carry):
        for a in range(8):
            values = [flux[field, a * 64 + 8 * b : a * 64 + 8 * b + 8, :] for b in range(8)]
            for i in range(8):
                place = slice(a * 64 + 8 * i, a * 64 + 8 * i + 8)
                total = before_ref[field, place, :]
                for j in range(8):
                    total = total + float(deriv[i, j]) * values[j]
                volume_ref[field, place, :] = total
        return carry

    lax.fori_loop(0, 5, body, 0)


def gather_kernel(split_ref, mortar_ref, face_ref, gather_ref):
    picked = jnp.dot(split_ref[...], own_choice(mortar_ref, face_ref), preferred_element_type=F32)
    gather_ref[0:ROWS, :] = halves(picked, ROWS)
    gather_ref[ROWS : ROWS + 16, :] = picked[2 * ROWS : 2 * ROWS + 16]


def third_kernel(turn_ref, state_ref, before_ref, mix_ref, volume_ref, flux):
    axis_flux(state_ref, 2, flux)
    for half in range(2):
        part = slice(256 * half, 256 * half + 256)
        mixed = jnp.dot(
            mix_ref[...],
            jnp.concatenate([flux[field, part, :] for field in range(5)], axis=1),
            precision=HIGHEST,
            preferred_element_type=F32,
        )
        for field in range(5):
            volume_ref[field, part, :] = before_ref[field, part, :] + mixed[:, field * ELEMS : (field + 1) * ELEMS]


def trace_flux(fields, normal):
    density, one, two, three, energy = fields
    inverse = 1.0 / density
    press = (GAMMA - 1.0) * (energy - 0.5 * (one * one + two * two + three * three) * inverse)
    flow = one * normal[0] + two * normal[1] + three * normal[2]
    speed = flow * inverse
    return [
        flow,
        one * speed + press * normal[0],
        two * speed + press * normal[1],
        three * speed + press * normal[2],
        (energy + press) * speed,
    ]


def child_select(stack, index):
    lanes = slice(index * ELEMS, (index + 1) * ELEMS)
    lane = iota((64, ELEMS), 1)
    value = stack[192:256, lanes]
    for child in (2, 1, 0):
        value = jnp.where(lane < 32 * (child + 1), stack[64 * child : 64 * child + 64, lanes], value)
    return value


def by_child(matrix_ref, values):
    high, mid = split2(jnp.concatenate(values, axis=1))
    stack = jnp.dot(
        matrix_ref[...], jnp.concatenate([high, mid, high, mid], axis=0), preferred_element_type=F32
    )
    return [child_select(stack, index) for index in range(len(values))]


def face_kernel(
    devices, turn_ref, gather_ref, i0, i2, i3, i4, mortar_ref, face_ref, project_ref, back_ref,
    corr_ref, chip_ref, raw_ref, far_ref, pool_ref
):
    partners = partner_of(lax.axis_index("sfc"), devices)
    incoming = gather_blocks(devices, i0, i2, i3, i4, slice(0, 384))
    remote = remote_choice(mortar_ref, face_ref, partners)
    arrived = jnp.concatenate(
        incoming + [jnp.zeros((ELEMS - PEERS * WIDTH, 384), F32)], axis=0
    ).T
    high, mid = split2(arrived[:ROWS])
    picked = jnp.dot(
        jnp.concatenate([high, mid, arrived[ROWS : ROWS + 16].astype(BF16)], axis=0),
        remote,
        preferred_element_type=F32,
    )
    pool_ref[0:ROWS, :] = gather_ref[0:ROWS, :] + halves(picked, ROWS)
    normals = gather_ref[ROWS : ROWS + 8, :] + picked[2 * ROWS : 2 * ROWS + 8]
    sides = []
    for side in range(4):
        lanes = slice(side * ELEMS, (side + 1) * ELEMS)
        fields = [pool_ref[64 * field : 64 * field + 64, lanes] for field in range(5)]
        normal = [normals[axis : axis + 1, lanes] for axis in range(3)]
        sides.append((fields, trace_flux(fields, normal)))
    (large_u, large_f), (left_u, left_f), (child_u, child_f), (right_u, right_f) = sides
    spread = by_child(project_ref, large_u + large_f)
    steady = [0.5 * (spread[5 + k] - child_f[k]) for k in range(5)]
    moving = [0.5 * (spread[k] - child_u[k]) for k in range(5)]
    folded = by_child(back_ref, steady + moving)
    for k in range(5):
        rows = slice(64 * k, 64 * k + 64)
        more = slice(ROWS + 64 * k, ROWS + 64 * k + 64)
        corr_ref[rows, 0:128] = folded[k] - 0.25 * large_f[k]
        corr_ref[more, 0:128] = folded[5 + k]
        corr_ref[rows, 256:384] = -steady[k] - child_f[k]
        corr_ref[more, 256:384] = -moving[k]
        even = 0.5 * (left_f[k] - right_f[k])
        jump = 0.5 * (left_u[k] - right_u[k])
        corr_ref[rows, 128:256] = even - left_f[k]
        corr_ref[more, 128:256] = jump
        corr_ref[rows, 384:512] = -even - right_f[k]
        corr_ref[more, 384:512] = -jump
    back = sum(dot_nt(part, remote) for part in split2(corr_ref[...])).T
    chip_ref[...] = back[0 : 2 * WIDTH]
    raw_ref[...] = back[2 * WIDTH : 4 * WIDTH]
    far_ref[...] = back[4 * WIDTH : 5 * WIDTH]


def reply_kernel(turn_ref, last_ref, raw_ref, chip_ref, pair_ref, next_ref, best_ref):
    best = jnp.maximum(turn_ref[...], last_ref[...])
    best_ref[...] = best
    pair_ref[0:WIDTH, 0 : 2 * ROWS] = raw_ref[0:WIDTH, :]
    next_ref[0:WIDTH, 0 : 2 * ROWS] = raw_ref[WIDTH : 2 * WIDTH, :]
    for ref in (pair_ref, next_ref):
        ref[WIDTH : 2 * WIDTH, 0 : 2 * ROWS] = chip_ref[WIDTH : 2 * WIDTH, :]
    for ref in (pair_ref, next_ref):
        for k in range(ref.shape[0] // 8):
            ref[8 * k : 8 * k + 8, 2 * ROWS :] = best


def lift_kernel(
    turn_ref, corr_ref, mortar_ref, face_ref, volume_ref, register_ref, scale_ref, steady_ref, rate_ref
):
    chosen = own_choice(mortar_ref, face_ref)
    scale = scale_ref[0:1, :]
    for field in range(5):
        steady_ref[field] = SECTION_A * register_ref[field]
        rate_ref[field] = -scale * volume_ref[field]
    parts = split2(corr_ref[...])
    layers = sum(dot_nt(part, chosen) for part in parts)
    lift = -LIFT * scale
    for face in range(6):
        lanes = slice(face * ELEMS, (face + 1) * ELEMS)
        for field in range(5):
            add_layer(rate_ref, field, face, lift * layers[64 * field : 64 * field + 64, lanes])
            add_layer(
                steady_ref, field, face, lift * layers[ROWS + 64 * field : ROWS + 64 * field + 64, lanes]
            )


def lift_rows(parts, lift):
    total = parts[0:64] + parts[64:128]
    return [lift * total[:, face * ELEMS : (face + 1) * ELEMS] for face in range(6)]


def finish_kernel(
    devices, steady_ref, rate_ref, state_ref, i0, i3, i4, i2, fast_ref, chosen_ref, scale_ref,
    state_hbm, register_hbm, state_out, register_out, sems
):
    fast = fast_ref[...]
    for ref in (i2, i3):
        fast = jnp.maximum(fast, ref[0:8, 2 * ROWS :])
    fast = jnp.where(iota((8, ELEMS), 1) < 80, 0.0, fast)
    lam = jnp.max(jnp.max(fast, axis=0, keepdims=True), axis=1, keepdims=True)
    inverse = 1.0 / lam
    lift = -LIFT * scale_ref[0:1, :] * inverse
    chosen = chosen_ref[...]
    arrived = jnp.concatenate(
        [
            block[:, 0:ROWS] + lam * block[:, ROWS : 2 * ROWS]
            for block in gather_blocks(devices, i0, i2, i3, i4, slice(0, 2 * ROWS))
        ]
        + [jnp.zeros((ELEMS - PEERS * WIDTH, ROWS), F32)],
        axis=0,
    ).T
    high, mid = split2(arrived)
    copies = []
    for field in range(5):
        rows = slice(64 * field, 64 * field + 64)
        parts = jnp.dot(jnp.concatenate([high[rows], mid[rows]], axis=0), chosen, preferred_element_type=F32)
        layers = lift_rows(parts, lift)
        register_out[field] = steady_ref[field] + inverse * rate_ref[field]
        for face in range(6):
            add_layer(register_out, field, face, layers[face])
        copies.append(pltpu.make_async_copy(register_out.at[field], register_hbm.at[field], sems.at[2 * field]))
        copies[-1].start()
        state_out[field] = state_ref[field] + SECTION_B * register_out[field]
        copies.append(pltpu.make_async_copy(state_out.at[field], state_hbm.at[field], sems.at[2 * field + 1]))
        copies[-1].start()
    for copy in copies:
        copy.wait()


VMEM = pl.BlockSpec(memory_space=pltpu.VMEM)
HBM = pl.BlockSpec(memory_space=pltpu.HBM)


def call(kernel, name, outs, specs, cost, scratch=(), out_specs=None):
    return pl.pallas_call(
        kernel,
        name=name,
        out_shape=[jax.ShapeDtypeStruct(shape, dtype) for shape, dtype in outs],
        in_specs=specs,
        out_specs=out_specs or [VMEM] * len(outs),
        scratch_shapes=list(scratch),
        compiler_params=pltpu.CompilerParams(vmem_limit_bytes=40 * 1024 * 1024),
        cost_estimate=pl.CostEstimate(flops=cost[0], bytes_accessed=cost[1], transcendentals=0),
    )


def per_device(state, register, metric, counts, send_slots, mortar_refs, face_refs):
    devices = lax.axis_size("sfc")
    deriv, project, back, mix = node_tables()
    metric = metric.reshape(1, ELEMS)
    sends, mortars, faces = send_slots.T, mortar_refs.T, face_refs.T
    pairs = pairings(devices)
    cube = (5, 512, ELEMS)
    flux = [pltpu.VMEM(cube, F32)]

    def exchange(value, name):
        return lax.ppermute(value, "sfc", pairs[name])

    one, two, three = [((k * WIDTH, 384), F32) for k in (1, 2, 3)]
    row = ((8, ELEMS), F32)
    split, speed = call(
        table_kernel, "table", [((2 * ROWS + 16, SLOTS), BF16), row], [VMEM], (100_000_000, 3_000_000)
    )(state)
    chip, raw, fast, scale, chosen = call(
        functools.partial(send_kernel, devices), "send", [two, three, row, row, ((ELEMS, SLOTS), BF16)], [VMEM] * 5,
        (200_000_000, 2_000_000),
    )(split, speed, counts.reshape(1, 1), sends, metric)
    chip = exchange(chip, "chip")
    onward, far, fast = call(relay_kernel, "relay", [two, one, row], [VMEM] * 3, (0, 200_000))(raw, chip, fast)
    far = exchange(far, "far")
    onward = exchange(onward, "next")
    (gathered,) = call(
        gather_kernel, "gather", [((ROWS + 16, 512), F32)], [VMEM] * 3, (1_000_000_000, 2_000_000)
    )(split, mortars, faces)
    pair, fast = call(pair_kernel, "pair", [two, row], [VMEM] * 5, (0, 200_000))(gathered, raw, chip, far, fast)
    pair = exchange(pair, "pair")
    fast = jnp.maximum(fast, pair[0:8, 256:384])
    came = exchange(fast, "y_first")
    (volume,) = call(
        functools.partial(first_kernel, deriv), "volume_first", [(cube, F32)], [VMEM] * 2,
        (1_000_000_000, 2_600_000), flux,
    )(fast, state)
    fast = jnp.maximum(fast, came)
    came = exchange(fast, "y_second")
    corrections, chip, raw, far = call(
        functools.partial(face_kernel, devices), "faces",
        [
            ((2 * ROWS, 512), F32), ((2 * WIDTH, 2 * ROWS), F32), ((2 * WIDTH, 2 * ROWS), F32),
            ((WIDTH, 2 * ROWS), F32),
        ],
        [VMEM] * 10, (1_000_000_000, 3_000_000), [pltpu.VMEM((ROWS, 512), F32)],
    )(fast, gathered, chip, pair, onward, far, mortars, faces, stack_terms(project), stack_terms(back))
    fast = jnp.maximum(fast, came)
    came = exchange(fast, "z_first")
    chip = exchange(chip, "chip")
    far = exchange(far, "far")
    (volume,) = call(
        functools.partial(second_kernel, deriv), "volume_second", [(cube, F32)], [VMEM] * 3,
        (1_000_000_000, 3_900_000), flux,
    )(fast, state, volume)
    wide = 2 * ROWS + ELEMS
    pair, onward, fast = call(
        reply_kernel, "reply",
        [((2 * WIDTH, wide), F32)] * 2 + [row], [VMEM] * 4, (0, 500_000),
    )(fast, came, raw, chip)
    onward = exchange(onward, "next")
    pair = exchange(pair, "pair")
    (volume,) = call(
        third_kernel, "volume_third", [(cube, F32)], [VMEM] * 4, (1_000_000_000, 6_000_000), flux,
    )(fast, state, volume, jnp.asarray(mix))
    steady, rate = call(
        lift_kernel, "lift", [(cube, F32)] * 2, [VMEM] * 7, (1_500_000_000, 6_000_000)
    )(fast, corrections, mortars, faces, volume, register, scale)
    return tuple(
        call(
            functools.partial(finish_kernel, devices), "finish", [(cube, F32)] * 2,
            [VMEM] * 10, (200_000_000, 6_000_000),
            [pltpu.VMEM(cube, F32)] * 2 + [pltpu.SemaphoreType.DMA((10,))], [HBM] * 2,
        )(steady, rate, state, chip, onward, far, pair, fast, chosen, scale)
    )


def solution(mesh):
    return jax.shard_map(
        per_device,
        mesh=mesh,
        in_specs=(
            P(None, None, "sfc"),
            P(None, None, "sfc"),
            P("sfc"),
            P("sfc"),
            P("sfc", None),
            P("sfc", None),
            P("sfc", None),
        ),
        out_specs=(P(None, None, "sfc"), P(None, None, "sfc")),
        check_vma=False,
    )
```
